128 devices in a mesh: dev: 128 (over y, x, z, core).
Axes of the slice: x: 4, y: 4, z: 4, core: 2. Of those that a mesh axis runs over, the one named last changes fastest.
Arguments:
- node_table: bfloat16 [1048576, 256], P('dev'), may hold values from -6 to 6
- owners: int32 [65536, 2], P('dev'), may hold values from 0 to 127, all different within a row; in each aligned block of 512 rows (0 to 511, 512 to 1023, ...) at most 12 rows name the same one
- local_rows: int32 [65536, 2], P('dev'), may hold values from 0 to 8191
- labels: int32 [65536], P('dev'), may hold values from 0 to 1
- w_first: bfloat16 [768, 512], replicated, may hold values from -0.21875 to 0.21875
- bias_first: float32 [512], replicated, may hold values from -3 to 3
- w_second: bfloat16 [512, 512], replicated, may hold values from -0.25 to 0.25
- bias_second: float32 [512], replicated, may hold values from -3 to 3
- w_head: bfloat16 [512], replicated, may hold values from -0.25 to 0.25
- head_bias: float32 [1], replicated, may hold values from -1 to 1
Outputs:
- new_table: float32 [1048576, 256], P('dev')
- grad_first: float32 [768, 512], replicated
- grad_second: float32 [512, 512], replicated
- grad_small: float32 [3, 512], replicated
The draws below stay inside these ranges and needn't reach their ends.
Inputs may be any that keep to these rules, and one draw needn't show every extreme that they name: Within each device's 512 pairs no device owns more than 12 endpoints, and some device owns exactly 12; the two endpoints of a pair have different owners.
All inputs are finite; a program needn't handle non-finite values.
Results may differ from the reference program's by a relative error of at most 0.01.
The reference program's roundings to bfloat16 on the way (of `product`, `features`, `hidden_first`, `hidden_second`, `delta_second` and `delta_first`) count: a program that leaves them out, or rounds other values in their place, can miss the bound.
Values may be sent and summed in bfloat16 or wider, within the bound.
A program may use at most 128 MiB of HBM per device.

```python
import math
import jax
import jax.numpy as jnp
import numpy as np

E = 256
H = 512
IN = 768
ROWS_DEV = 8192
PAIRS_DEV = 512
CAP = 12
NODES = 1048576
PAIRS = 65536
N_DEV = 128


def touch_ends(values, rng, least, largest):
    place = [jax.random.randint(jax.random.fold_in(rng, axis), (), 0, length) for axis, length in enumerate(values.shape)]
    widest = values.shape.index(max(values.shape))
    beside = place[:widest] + [(place[widest] + 1) % values.shape[widest]] + place[widest + 1:]
    return values.at[tuple(place)].set(least).at[tuple(beside)].set(largest)


def level_of(stream_key, dims, shards, low, largest):
    loudness, own = 1.0, jax.random.fold_in(stream_key, 6)
    for axis_at, blocks in shards:
        draws = jnp.exp(jax.random.uniform(jax.random.fold_in(own, axis_at), (blocks,), jnp.float32, low / len(shards), largest / len(shards)))
        loudness = loudness * jnp.repeat(draws, dims[axis_at] // blocks).reshape([-1 if axis == axis_at else 1 for axis in range(len(dims))])
    return loudness


def cumulative_ranks(amount, lean):
    weights = [(1 << 20) // math.isqrt(grade ** lean) + 1 for grade in range(1, amount + 1)]
    scale = 1 + sum(weights) // (1 << 30)
    return np.cumsum(np.array([max(1, weight // scale) for weight in weights]))


def skewed_ids(rng, shape, amount, lean):
    table = cumulative_ranks(amount, lean)
    ticket = jax.random.randint(jax.random.fold_in(rng, 1), shape, 0, int(table[amount - 1]))
    rank = jnp.searchsorted(jnp.asarray(table, jnp.int32), ticket, side="right")
    return jax.random.permutation(jax.random.fold_in(rng, 2), amount)[rank].astype(jnp.int32)


def routed_block(rng, own, number, rows, amount, top, most, lean):
    order = jax.random.permutation(rng, amount)
    heavy_load, ordinary = load_shares(amount, rows * top, most, lean, True), load_shares(amount, rows * top, most, lean, False)
    places = jnp.arange(amount)

    def named(lengths, turn):
        used = int((lengths > 0).sum())
        fixed = max(1, used // 4)
        moved = fixed + (places - fixed + turn * (used - fixed)) % max(1, amount - fixed)
        return jnp.zeros((amount,), jnp.int32).at[order[jnp.where(places < fixed, places, moved)]].set(jnp.asarray(lengths, jnp.int32))

    lengths = jnp.where(number % 4 == 0, named(heavy_load, number // 4), named(ordinary, number - number // 4 - 1))
    mixed = jax.random.permutation(jax.random.fold_in(own, 3), amount)
    giver, taker = mixed[0:amount // 2 * 2:2], mixed[1:amount // 2 * 2:2]
    room = jnp.minimum(lengths[giver] - 1, most - lengths[taker]) // 2
    room = jnp.where((giver == order[0]) | (taker == order[0]) | (lengths[taker] == 0), 0, jnp.maximum(room, 0))
    moved = jax.random.randint(jax.random.fold_in(own, 4), (amount // 2,), 0, 1 << 20) % (room + 1)
    lengths = lengths.at[giver].add(-moved).at[taker].add(moved)
    items = jnp.searchsorted(jnp.cumsum(lengths), jnp.arange(rows * top), side="right").astype(jnp.int32)
    table = items.reshape(top, rows).T
    table = table[jax.random.permutation(jax.random.fold_in(own, 1), rows)]
    turn = jax.random.randint(jax.random.fold_in(own, 2), (rows, 1), 0, top)
    return jnp.take_along_axis(table, (jnp.arange(top)[None, :] + turn) % top, axis=1)


def load_shares(count, total, bound, skew, full):
    loads = [(1 << 20) // math.isqrt(rank ** skew) + 1 for rank in range(1, count + 1)]
    largest = bound if full else min(bound, max(-(-total // count), total * loads[0] // sum(loads)))
    least = 1 if total - largest >= count - 1 else 0
    holding, spare = [largest] + [least] * (count - 1), total - largest - least * (count - 1)
    while spare > 0:
        free = [i for i in range(1, count) if holding[i] < largest] or [i for i in range(1, count) if holding[i] < bound]
        mass, remaining = sum([loads[i] for i in free]), spare
        for i in free:
            extra = min(bound - holding[i], max(1, remaining * loads[i] // mass), spare)
            holding[i] = holding[i] + extra
            spare = spare - extra
    return np.array(holding)


def bell_draw(key, extent, width, reach, split=(), dtype=jnp.bfloat16):
    array = width * jax.random.normal(key, extent, jnp.float32)
    if split:
        array = array * level_of(key, extent, split, -0.22, 0.18)
    return jnp.clip(array, -reach, reach).astype(dtype)


def setup_inputs(seed: int = 0) -> dict:
    splits = jax.random.split(jax.random.key(seed), 11)
    node_table = bell_draw(splits[0], (NODES, E), 1.0, 6.0, ((0, 128),))
    owners_keys = jax.random.split(jax.random.fold_in(splits[1], 1), PAIRS // PAIRS_DEV)
    owners_turns = jax.random.permutation(jax.random.fold_in(splits[1], 3), PAIRS // PAIRS_DEV)
    owners = jax.vmap(lambda own, number: routed_block(jax.random.fold_in(splits[1], 2), own, number, PAIRS_DEV, N_DEV, 2, CAP, 2))(owners_keys, owners_turns).reshape((PAIRS, 2))
    local_rows = touch_ends(skewed_ids(splits[2], (PAIRS, 2), ROWS_DEV, 2), jax.random.fold_in(splits[2], 3), 0, ROWS_DEV - 1).astype(jnp.int32)
    labels = touch_ends(jax.random.randint(splits[3], (PAIRS,), 0, 2), jax.random.fold_in(splits[3], 1), 0, 1).astype(jnp.int32)
    w_first = bell_draw(splits[4], (IN, H), IN ** -0.5, 0.21875)
    bias_first = bell_draw(splits[5], (H,), 0.5, 3.0, (), jnp.float32)
    w_second = bell_draw(splits[6], (H, H), H ** -0.5, 0.25)
    bias_second = bell_draw(splits[7], (H,), 0.5, 3.0, (), jnp.float32)
    w_head = bell_draw(splits[8], (H,), H ** -0.5, 0.25)
    head_bias = jnp.clip(jax.random.uniform(splits[9], (1,), jnp.float32, -1.0, 1.0), -1.0, 1.0)
    return {"node_table": node_table, "owners": owners, "local_rows": local_rows, "labels": labels, "w_first": w_first, "bias_first": bias_first, "w_second": w_second, "bias_second": bias_second, "w_head": w_head, "head_bias": head_bias}


def reference(node_table, owners, local_rows, labels, w_first, bias_first, w_second, bias_second, w_head, head_bias):
    row_ids = (owners * ROWS_DEV + local_rows).astype(jnp.int32)
    first_rows = node_table[row_ids[:, 0]]
    second_rows = node_table[row_ids[:, 1]]
    product = (first_rows.astype(jnp.float32) * second_rows.astype(jnp.float32)).astype(jnp.bfloat16)
    features = jnp.concatenate([first_rows, second_rows, product], axis=1)
    pre_first = jnp.dot(features, w_first, preferred_element_type=jnp.float32) + bias_first
    hidden_first = jnp.maximum(pre_first, 0.0).astype(jnp.bfloat16)
    pre_second = jnp.dot(hidden_first, w_second, preferred_element_type=jnp.float32) + bias_second
    hidden_second = jnp.maximum(pre_second, 0.0).astype(jnp.bfloat16)
    logit = jnp.dot(hidden_second, w_head, preferred_element_type=jnp.float32) + head_bias[0]
    dlogit = jax.nn.sigmoid(logit) - labels.astype(jnp.float32)
    delta_second = (dlogit[:, None] * w_head.astype(jnp.float32)[None, :] * (pre_second > 0)).astype(jnp.bfloat16)
    delta_first = (jnp.dot(delta_second, w_second.T, preferred_element_type=jnp.float32) * (pre_first > 0)).astype(jnp.bfloat16)
    grad_input = jnp.dot(delta_first, w_first.T, preferred_element_type=jnp.float32)
    grad_one = grad_input[:, :E] + grad_input[:, 2 * E:] * second_rows.astype(jnp.float32)
    grad_two = grad_input[:, E:2 * E] + grad_input[:, 2 * E:] * first_rows.astype(jnp.float32)
    grad_first = jnp.dot(features.T, delta_first, preferred_element_type=jnp.float32)
    grad_second = jnp.dot(hidden_first.T, delta_second, preferred_element_type=jnp.float32)
    grad_small = jnp.stack([
        jnp.sum(delta_first.astype(jnp.float32), axis=0),
        jnp.sum(delta_second.astype(jnp.float32), axis=0),
        jnp.dot(dlogit, hidden_second.astype(jnp.float32)),
    ])
    row_grad = jnp.zeros((NODES, E), jnp.float32)
    row_grad = row_grad.at[row_ids[:, 0]].add(grad_one).at[row_ids[:, 1]].add(grad_two)
    new_table = node_table.astype(jnp.float32) - 8.0 * row_grad
    return new_table, grad_first, grad_second, grad_small
```

```python
import jax
import jax.numpy as jnp
from jax import lax
from jax.experimental import pallas as pl
from jax.experimental.pallas import tpu as pltpu
from jax.sharding import PartitionSpec as P

F32, BF16, I32 = jnp.float32, jnp.bfloat16, jnp.int32
MESH = pl.DeviceIdType.MESH
DEVS, CAP = 128, 12
SLOTS = DEVS * CAP
PAIRS, EMB, HID, IN = 512, 256, 512, 768
ROWS = 8192
UNITS, PIECE = 672, 7
UNITS_FIRST, UNITS_SECOND = 384, 256


def nt(a, b):
    return lax.dot_general(a, b, (((1,), (1,)), ((), ())), preferred_element_type=F32)


def tn(a, b):
    return lax.dot_general(a, b, (((0,), (0,)), ((), ())), preferred_element_type=F32)


def dot(a, b):
    return jnp.dot(a, b, preferred_element_type=F32)


def device(y, x, z, c):
    return ((y * 4 + x) * 4 + z) * 2 + c


def far_first(k):
    return 2 + k - 3 * (k // 2) - 2 * (k // 3)


ZC_ORDER = (4, 5, 2, 3, 6, 7, 1, 0)


def remote(src, dst, send, recv, to):
    return pltpu.make_async_remote_copy(
        src_ref=src, dst_ref=dst, send_sem=send, recv_sem=recv, device_id=(to,), device_id_type=MESH
    )


def step_kernel(
    owners, rows, labels, table, w_first, bias_first, w_second, bias_second, w_head, head_bias,
    incoming, row_ids, gathered,
    tab16, tab32, w1, w2,
    ask_send, ask_mid, ask_mid2, ask_got, ask_smem, slot_row, label_col,
    pick, place, stage, rows_send, rows_got, pack, fetched,
    feat, hid1, del1, del2, one_hot_grads, out32, grads_send,
    local32, local16, got_core, sum0, half0, got1, sum1, half1, got2, half2, got3,
    load_sem, ask1_s, ask1_r, ask2_s, ask2_r, smem_sem, row_s, row_r, grad_s, grad_r,
    core_s, core_r, rs1_s, rs1_r, rs2_s, rs2_r, x3_s, x3_r, ag2_s, ag2_r, ag1_s, ag1_r, agc_s, agc_r,
):
    me = lax.axis_index("dev")
    my, mx, mz, mc = me // 32, me // 8 % 4, me // 2 % 4, me % 2

    def zc_plus(j):
        return device(my, mx, (mz + j // 2) % 4, (mc + j) % 2)

    def yx_plus(i):
        return device((my + i // 4) % 4, (mx + i) % 4, mz, mc)

    def minus(i, j):
        return device((my + 4 - i // 4) % 4, (mx + 4 - i % 4) % 4, (mz + 4 - j // 2) % 4, (mc + j) % 2)

    def plus(i, j):
        return device((my + i // 4) % 4, (mx + i) % 4, (mz + j // 2) % 4, (mc + j) % 2)

    barrier = pltpu.get_barrier_semaphore()
    for j in range(1, 8):
        pl.semaphore_signal(barrier, inc=1, device_id=(zc_plus(j),), device_id_type=MESH)
    for i in range(1, 16):
        pl.semaphore_signal(barrier, inc=1, device_id=(yx_plus(i),), device_id_type=MESH)

    loads = [
        pltpu.make_async_copy(
            table.at[pl.ds(k * 2048, 2048)], tab16.at[pl.ds(k * 2048, 2048)], load_sem.at[k]
        )
        for k in range(4)
    ] + [
        pltpu.make_async_copy(w_first, w1, load_sem.at[4]),
        pltpu.make_async_copy(w_second, w2, load_sem.at[5]),
    ]
    for load in loads:
        load.start()

    own = owners[...]
    d_y = ((own >> 5) - my) & 3
    d_x = ((own >> 3) - mx) & 3
    d_z = ((own >> 1) - mz) & 3
    d_c = (own - mc) & 1
    d_yx, d_zc = d_y * 4 + d_x, d_z * 2 + d_c
    ask_bucket, bucket = d_zc * 16 + d_yx, d_yx * 8 + d_zc
    row = rows[...]
    row_hi, row_lo = (row >> 6).astype(F32), (row & 63).astype(F32)
    sub = lax.broadcasted_iota(I32, (128, 128), 0)
    lane = lax.broadcasted_iota(I32, (128, 128), 1)
    earlier = jnp.where(sub < lane, 1.0, 0.0).astype(BF16)
    ones = jnp.ones((128, 128), BF16)
    carry = jnp.zeros((128, 128), F32)
    ask_hi = jnp.zeros((128, 128), F32)
    ask_lo = jnp.zeros((128, 128), F32)
    for b in range(8):
        side, cols = b // 4, slice(128 * (b % 4), 128 * (b % 4) + 128)
        hot32 = jnp.where(sub == ask_bucket[side : side + 1, cols], 1.0, 0.0)
        hot = hot32.astype(BF16)
        before = dot(hot, earlier) + carry
        carry = carry + dot(hot, ones)
        nth = jnp.sum(hot32 * before, axis=0, keepdims=True).astype(I32)
        at_nth = sub == nth
        hi = jnp.where(at_nth, row_hi[side : side + 1, cols], 0.0).astype(BF16)
        lo = jnp.where(at_nth, row_lo[side : side + 1, cols], 0.0).astype(BF16)
        ask_hi = ask_hi + nt(hot, hi)
        ask_lo = ask_lo + nt(hot, lo)
        slot_row[b] = bucket[side : side + 1, cols] * CAP + nth
    ask = (ask_hi * 64.0 + ask_lo).astype(I32)
    for j in range(8):
        ask_send[j] = ask[16 * j : 16 * j + 16]

    pl.semaphore_wait(barrier, 22)
    asks = []
    for j in range(1, 8):
        copy = remote(ask_send.at[j], ask_mid.at[j], ask1_s.at[j], ask1_r.at[j], zc_plus(j))
        copy.start()
        asks.append(copy)
    ask_mid[0] = ask_send[0]

    for k in range(4):
        loads[k].wait()

        @pl.loop(0, 32)
        def _(t):
            at = pl.ds(pl.multiple_of(k * 2048 + t * 64, 64), 64)
            tab32[at, :] = tab16[at, :].astype(F32)

    for copy in asks:
        copy.wait_recv()
    for i in range(16):
        for j in range(8):
            ask_mid2[i, pl.ds(j, 1), :] = ask_mid[j, pl.ds(i, 1), :]
    asks2 = []
    for i in range(1, 16):
        copy = remote(ask_mid2.at[i], ask_got.at[i], ask2_s.at[i], ask2_r.at[i], yx_plus(i))
        copy.start()
        asks2.append(copy)
    ask_got[0] = ask_mid2[0]

    for b in range(8):
        slot_b = slot_row[b]
        column = jnp.transpose(jnp.broadcast_to(slot_b.astype(F32), (128, 128))).astype(I32)

        @pl.loop(0, 12)
        def _(k):
            at = pl.ds(pl.multiple_of(k * 128, 128), 128)
            pick[128 * b : 128 * b + 128, at] = jnp.where(column == lane + k * 128, 1.0, 0.0).astype(BF16)
            place[at, 128 * b : 128 * b + 128] = jnp.where(sub + k * 128 == slot_b, 1.0, 0.0).astype(BF16)

    for b in range(4):
        part = labels[:, 128 * b : 128 * b + 128].astype(F32)
        label_col[128 * b : 128 * b + 128, :] = jnp.transpose(jnp.broadcast_to(part, (128, 128)))

    for copy in asks2:
        copy.wait_recv()
    to_smem = pltpu.make_async_copy(ask_got, ask_smem, smem_sem)
    to_smem.start()
    row_ids[...] = ask_got[...]
    to_smem.wait()

    def look_up(i, j, out):
        for c in range(CAP):
            asked = jnp.clip(ask_smem[i, j, c], 0, ROWS - 1)
            stage[j, pl.ds(c, 1), :] = tab32[pl.ds(asked, 1), :]
        for q in range(3):
            out[q] = stage[j, 4 * q : 4 * q + 4, :].astype(BF16)

    def send_rows(i, j):
        r = i * 8 + j
        look_up(i, j, rows_send.at[r])
        remote(rows_send.at[r], rows_got.at[r], row_s, row_r, minus(i, j)).start()

    def rows_of(t, carry):
        i = far_first(t // 4) * 4 + far_first(t % 4)
        for j in ZC_ORDER:
            send_rows(i, j)
        return carry

    lax.fori_loop(0, 15, rows_of, 0)
    for j in ZC_ORDER[:-1]:
        send_rows(0, j)
    look_up(0, 0, rows_got.at[0])

    for k in (4, 5):
        loads[k].wait()
    rest = pl.ds(1, DEVS - 1)
    pltpu.make_async_copy(rows_got.at[rest], rows_got.at[rest], row_r).wait()

    @pl.loop(0, 32)
    def _(g):
        for a in range(4):
            for q in range(3):
                pack[12 * a + 4 * q : 12 * a + 4 * q + 4, :] = rows_got[g * 4 + a, q].astype(F32)
        fetched[pl.ds(pl.multiple_of(g * 48, 16), 48), :] = pack[...].astype(BF16)

    local32[...] = jnp.zeros_like(local32)
    head = w_head[...].astype(F32)
    small = [jnp.zeros((1, HID), F32)] * 3
    for m in range(2):
        at = slice(256 * m, 256 * m + 256)
        first = dot(pick[256 * m : 256 * m + 256, :], fetched[...])
        second = dot(pick[PAIRS + 256 * m : PAIRS + 256 * m + 256, :], fetched[...])
        feat[at, 0:EMB] = first.astype(BF16)
        feat[at, EMB : 2 * EMB] = second.astype(BF16)
        feat[at, 2 * EMB :] = (first * second).astype(BF16)
        pre_first = dot(feat[at, :], w1[...]) + bias_first[...]
        hid1[at, :] = jnp.maximum(pre_first, 0.0).astype(BF16)
        pre_second = dot(hid1[at, :], w2[...]) + bias_second[...]
        hidden_second = jnp.maximum(pre_second, 0.0).astype(BF16).astype(F32)
        logit = jnp.sum(hidden_second * head, axis=1, keepdims=True) + head_bias[0]
        dlogit = 1.0 / (1.0 + jnp.exp(-logit)) - label_col[at, 0:1]
        delta_second = jnp.where(pre_second > 0, dlogit * head, 0.0).astype(BF16)
        del2[at, :] = delta_second
        delta_first = jnp.where(pre_first > 0, nt(delta_second, w2[...]), 0.0).astype(BF16)
        del1[at, :] = delta_first
        small = [
            small[0] + jnp.sum(delta_first.astype(F32), axis=0, keepdims=True),
            small[1] + jnp.sum(delta_second.astype(F32), axis=0, keepdims=True),
            small[2] + jnp.sum(hidden_second * dlogit, axis=0, keepdims=True),
        ]

    def put(unit, value):
        local32[unit] = value
        local16[unit] = value.astype(BF16)

    for block in range(3):
        grad = tn(feat[:, 256 * block : 256 * block + 256], del1[...])
        for t in range(32):
            for c in range(4):
                put(block * 128 + t * 4 + c, grad[8 * t : 8 * t + 8, 128 * c : 128 * c + 128])
    for block in range(2):
        grad = tn(hid1[:, 256 * block : 256 * block + 256], del2[...])
        for t in range(32):
            for c in range(4):
                put(
                    UNITS_FIRST + block * 128 + t * 4 + c,
                    grad[8 * t : 8 * t + 8, 128 * c : 128 * c + 128],
                )
    for c in range(4):
        for k in range(3):
            local32[640 + c, k : k + 1, :] = small[k][:, 128 * c : 128 * c + 128]
        local16[640 + c] = local32[640 + c].astype(BF16)
    for u in range(644, UNITS):
        local16[u] = jnp.zeros((8, 128), BF16)

    here = {"y": my, "x": mx, "z": mz}

    def along(axis, k):
        at = dict(here)
        at[axis] = (at[axis] + k) % 4
        return device(at["y"], at["x"], at["z"], mc)

    sibling = device(my, mx, mz, 1 - mc)
    lanes = (("y", "x", "z"), ("x", "z", "y"), ("z", "y", "x"))
    span1, span2 = 4 * PIECE, PIECE
    lane_units = 16 * PIECE

    def core_copy(l):
        at = pl.ds((1 - mc) * (UNITS // 2) + l * lane_units, lane_units)
        return remote(local16.at[at], got_core.at[l], core_s.at[l], core_r.at[l], sibling)

    def rs1_copy(l, k):
        axis = lanes[l][0]
        at = pl.ds((here[axis] + k) % 4 * span1, span1)
        return remote(half0.at[l, at], got1.at[l, k], rs1_s.at[l, k], rs1_r.at[l, k], along(axis, k))

    def rs2_copy(l, k):
        axis = lanes[l][1]
        at = pl.ds((here[axis] + k) % 4 * span2, span2)
        return remote(half1.at[l, at], got2.at[l, k], rs2_s.at[l, k], rs2_r.at[l, k], along(axis, k))

    def x3_copy(l, k):
        axis = lanes[l][2]
        return remote(half2.at[l], got3.at[l, here[axis]], x3_s.at[l, k], x3_r.at[l, k], along(axis, k))

    def unit_at(core, l, one, two=0):
        return core * (UNITS // 2) + l * lane_units + one * span1 + two * span2

    def ag2_copy(l, k):
        a, b = here[lanes[l][0]], here[lanes[l][1]]
        at = gathered.at[pl.ds(unit_at(mc, l, a, b), span2)]
        return remote(at, at, ag2_s.at[l, k], ag2_r.at[l, k], along(lanes[l][1], k))

    def ag1_copy(l, k):
        at = gathered.at[pl.ds(unit_at(mc, l, here[lanes[l][0]]), span1)]
        return remote(at, at, ag1_s.at[l, k], ag1_r.at[l, k], along(lanes[l][0], k))

    def agc_copy(l, k):
        at = gathered.at[pl.ds(unit_at(mc, l, (here[lanes[l][0]] + 4 - k) % 4), span1)]
        return remote(at, at, agc_s.at[l, k], agc_r.at[l, k], sibling)

    for l in range(3):
        core_copy(l).start()

    for m in range(2):
        at = slice(256 * m, 256 * m + 256)
        grad_input = nt(del1[at, :], w1[...])
        grad_product = grad_input[:, 2 * EMB :]
        grad_one = grad_input[:, :EMB] + grad_product * feat[at, EMB : 2 * EMB].astype(F32)
        grad_two = grad_input[:, EMB : 2 * EMB] + grad_product * feat[at, 0:EMB].astype(F32)
        one_hot_grads[256 * m : 256 * m + 256, :] = grad_one.astype(BF16)
        one_hot_grads[PAIRS + 256 * m : PAIRS + 256 * m + 256, :] = grad_two.astype(BF16)

    @pl.loop(0, 4)
    def _(k):
        at = pl.ds(pl.multiple_of(k * 384, 128), 384)
        out32[...] = dot(place[at, :], one_hot_grads[...])
        for r in range(32):
            for q in range(3):
                grads_send[k * 32 + r, q] = out32[12 * r + 4 * q : 12 * r + 4 * q + 4, :].astype(BF16)

    for l in range(3):
        core_copy(l).wait_recv()

        @pl.loop(0, 16)
        def _(t):
            at = pl.ds(t * PIECE, PIECE)
            total = (
                local32[pl.ds(mc * (UNITS // 2) + l * lane_units + t * PIECE, PIECE)]
                + got_core[l, at].astype(F32)
            )
            sum0[l, at] = total
            half0[l, at] = total.astype(BF16)

        for k in (2, 1, 3):
            rs1_copy(l, k).start()

    def grad_copy(i, j):
        r = i * 8 + j
        return remote(grads_send.at[r], incoming.at[r], grad_s, grad_r, plus(i, j))

    def grads_of(t, carry):
        i = far_first(t // 4) * 4 + far_first(t % 4)
        for j in ZC_ORDER:
            grad_copy(i, j).start()
        return carry

    lax.fori_loop(0, 15, grads_of, 0)
    for j in ZC_ORDER[:-1]:
        grad_copy(0, j).start()
    incoming[0] = grads_send[0]

    for l in range(3):
        for k in range(1, 4):
            rs1_copy(l, k).wait_recv()
        for t in range(4):
            at = pl.ds(t * PIECE, PIECE)
            total = sum0[l, pl.ds(here[lanes[l][0]] * span1 + t * PIECE, PIECE)]
            for k in range(1, 4):
                total = total + got1[l, k, at].astype(F32)
            sum1[l, at] = total
            half1[l, at] = total.astype(BF16)
        for k in (2, 1, 3):
            rs2_copy(l, k).start()
    for l in range(3):
        for k in range(1, 4):
            rs2_copy(l, k).wait_recv()
        total = sum1[l, pl.ds(here[lanes[l][1]] * span2, PIECE)]
        for k in range(1, 4):
            total = total + got2[l, k].astype(F32)
        half2[l] = total.astype(BF16)
        got3[l, here[lanes[l][2]]] = total.astype(BF16)
        for k in (2, 1, 3):
            x3_copy(l, k).start()
    for l in range(3):
        for k in range(1, 4):
            x3_copy(l, k).wait_recv()
        total = got3[l, 0].astype(F32)
        for a in range(1, 4):
            total = total + got3[l, a].astype(F32)
        gathered[pl.ds(unit_at(mc, l, here[lanes[l][0]], here[lanes[l][1]]), PIECE)] = total.astype(BF16)
        for k in (2, 1, 3):
            ag2_copy(l, k).start()
    for l in range(3):
        for k in range(1, 4):
            ag2_copy(l, k).wait_recv()
        for k in (2, 1, 3):
            ag1_copy(l, k).start()
        agc_copy(l, 0).start()
    for l in range(3):
        for k in (1, 3, 2):
            ag1_copy(l, k).wait_recv()
            agc_copy(l, k).start()
    for l in range(3):
        for k in range(4):
            agc_copy(l, k).wait_recv()
    pltpu.make_async_copy(incoming.at[rest], incoming.at[rest], grad_r).wait()

    for copy in asks + asks2:
        copy.wait_send()
    pltpu.make_async_copy(rows_send.at[rest], rows_send.at[rest], row_s).wait()
    pltpu.make_async_copy(grads_send.at[rest], grads_send.at[rest], grad_s).wait()
    for l in range(3):
        core_copy(l).wait_send()
        for k in range(1, 4):
            for copy in (rs1_copy, rs2_copy, x3_copy, ag2_copy, ag1_copy):
                copy(l, k).wait_send()
        for k in range(4):
            agc_copy(l, k).wait_send()


def step(owners, rows, labels, table, w_first, bias_first, w_second, bias_second, w_head, head_bias):
    vmem = pl.BlockSpec(memory_space=pltpu.VMEM)
    any_ = pl.BlockSpec(memory_space=pl.ANY)
    dma = pltpu.SemaphoreType.DMA
    scratch = [
        pltpu.VMEM((ROWS, EMB), BF16),
        pltpu.VMEM((ROWS, EMB), F32),
        pltpu.VMEM((IN, HID), BF16),
        pltpu.VMEM((HID, HID), BF16),
        pltpu.VMEM((8, 16, 128), I32),
        pltpu.VMEM((8, 16, 128), I32),
        pltpu.VMEM((16, 8, 128), I32),
        pltpu.VMEM((16, 8, 128), I32),
        pltpu.SMEM((16, 8, 128), I32),
        pltpu.VMEM((8, 1, 128), I32),
        pltpu.VMEM((PAIRS, 128), F32),
        pltpu.VMEM((2 * PAIRS, SLOTS), BF16),
        pltpu.VMEM((SLOTS, 2 * PAIRS), BF16),
        pltpu.VMEM((8, 16, EMB), F32),
        pltpu.VMEM((DEVS, 3, 4, EMB), BF16),
        pltpu.VMEM((DEVS, 3, 4, EMB), BF16),
        pltpu.VMEM((48, EMB), F32),
        pltpu.VMEM((SLOTS, EMB), BF16),
        pltpu.VMEM((PAIRS, IN), BF16),
        pltpu.VMEM((PAIRS, HID), BF16),
        pltpu.VMEM((PAIRS, HID), BF16),
        pltpu.VMEM((PAIRS, HID), BF16),
        pltpu.VMEM((2 * PAIRS, EMB), BF16),
        pltpu.VMEM((384, EMB), F32),
        pltpu.VMEM((DEVS, 3, 4, EMB), BF16),
        pltpu.VMEM((UNITS, 8, 128), F32),
        pltpu.VMEM((UNITS, 8, 128), BF16),
        pltpu.VMEM((3, 16 * PIECE, 8, 128), BF16),
        pltpu.VMEM((3, 16 * PIECE, 8, 128), F32),
        pltpu.VMEM((3, 16 * PIECE, 8, 128), BF16),
        pltpu.VMEM((3, 4, 4 * PIECE, 8, 128), BF16),
        pltpu.VMEM((3, 4 * PIECE, 8, 128), F32),
        pltpu.VMEM((3, 4 * PIECE, 8, 128), BF16),
        pltpu.VMEM((3, 4, PIECE, 8, 128), BF16),
        pltpu.VMEM((3, PIECE, 8, 128), BF16),
        pltpu.VMEM((3, 4, PIECE, 8, 128), BF16),
        dma((6,)), dma((8,)), dma((8,)), dma((16,)), dma((16,)), dma, dma, dma, dma, dma,
        dma((3,)), dma((3,)), dma((3, 4)), dma((3, 4)), dma((3, 4)), dma((3, 4)), dma((3, 4)), dma((3, 4)),
        dma((3, 4)), dma((3, 4)), dma((3, 4)), dma((3, 4)), dma((3, 4)), dma((3, 4)),
    ]
    return pl.pallas_call(
        step_kernel,
        out_shape=(
            jax.ShapeDtypeStruct((DEVS, 3, 4, EMB), BF16),
            jax.ShapeDtypeStruct((16, 8, 128), I32),
            jax.ShapeDtypeStruct((UNITS, 8, 128), BF16),
        ),
        in_specs=[vmem, vmem, vmem, any_, any_, vmem, any_, vmem, vmem, pl.BlockSpec(memory_space=pltpu.SMEM)],
        out_specs=(vmem, vmem, vmem),
        scratch_shapes=scratch,
        compiler_params=pltpu.CompilerParams(
            collective_id=0, has_side_effects=True, vmem_limit_bytes=56 << 20
        ),
        name="exchange_and_mlp",
    )(owners, rows, labels, table, w_first, bias_first, w_second, bias_second, w_head, head_bias)


BLOCK = 1024


def update_kernel(
    table, incoming, ids, units_first, units_second, units_small,
    new_table, grad_first, grad_second, grad_small,
    pack, grads,
):
    step = pl.program_id(0)

    @pl.when(step == 0)
    def _():
        @pl.loop(0, 32)
        def _(g):
            for a in range(4):
                for q in range(3):
                    pack[12 * a + 4 * q : 12 * a + 4 * q + 4, :] = incoming[g * 4 + a, q].astype(F32)
            grads[pl.ds(pl.multiple_of(g * 48, 16), 48), :] = pack[...].astype(BF16)

    for c in range(4):
        for t in range(12):
            grad_first[8 * t : 8 * t + 8, 128 * c : 128 * c + 128] = units_first[4 * t + c].astype(F32)
        for t in range(8):
            grad_second[8 * t : 8 * t + 8, 128 * c : 128 * c + 128] = units_second[4 * t + c].astype(F32)
        grad_small[:, 128 * c : 128 * c + 128] = units_small[c].astype(F32)[0:3]

    @pl.loop(0, BLOCK // 256)
    def _(t):
        at = pl.ds(pl.multiple_of(t * 256, 256), 256)
        here = lax.broadcasted_iota(I32, (256, SLOTS), 0) + (step * BLOCK + t * 256)
        hot = jnp.where(here == ids[...], 1.0, 0.0).astype(BF16)
        new_table[at, :] = table[at, :].astype(F32) - 8.0 * dot(hot, grads[...])


def update(table, incoming, ids, units):
    steps = ROWS // BLOCK
    return pl.pallas_call(
        update_kernel,
        grid=(steps,),
        in_specs=[
            pl.BlockSpec((BLOCK, EMB), lambda s: (s, 0)),
            pl.BlockSpec((DEVS, 3, 4, EMB), lambda s: (0, 0, 0, 0)),
            pl.BlockSpec((1, SLOTS), lambda s: (0, 0)),
            pl.BlockSpec((UNITS_FIRST // steps, 8, 128), lambda s: (s, 0, 0)),
            pl.BlockSpec((UNITS_SECOND // steps, 8, 128), lambda s: (12 + s, 0, 0)),
            pl.BlockSpec((4, 8, 128), lambda s: (160, 0, 0)),
        ],
        out_specs=(
            pl.BlockSpec((BLOCK, EMB), lambda s: (s, 0)),
            pl.BlockSpec((IN // steps, HID), lambda s: (s, 0)),
            pl.BlockSpec((HID // steps, HID), lambda s: (s, 0)),
            pl.BlockSpec((3, HID), lambda s: (0, 0)),
        ),
        out_shape=(
            jax.ShapeDtypeStruct((ROWS, EMB), F32),
            jax.ShapeDtypeStruct((IN, HID), F32),
            jax.ShapeDtypeStruct((HID, HID), F32),
            jax.ShapeDtypeStruct((3, HID), F32),
        ),
        scratch_shapes=[pltpu.VMEM((48, EMB), F32), pltpu.VMEM((SLOTS, EMB), BF16)],
        compiler_params=pltpu.CompilerParams(vmem_limit_bytes=48 << 20),
        name="scatter_update",
    )(table, incoming, ids, units, units, units)


def on_device(
    node_table, owners, local_rows, labels, w_first, bias_first, w_second, bias_second, w_head, head_bias
):
    incoming, row_ids, units = step(
        owners.T, local_rows.T, labels.reshape(1, PAIRS), node_table,
        w_first, bias_first.reshape(1, HID), w_second, bias_second.reshape(1, HID),
        w_head.reshape(1, HID), head_bias,
    )
    ids = row_ids[:, :, :CAP].reshape(1, SLOTS)
    return update(node_table, incoming, ids, units)


def solution(mesh):
    in_specs = (P("dev", None), P("dev", None), P("dev", None), P("dev"), P(), P(), P(), P(), P(), P())
    out_specs = (P("dev", None), P(), P(), P())
    return jax.shard_map(on_device, mesh=mesh, in_specs=in_specs, out_specs=out_specs, check_vma=False)
```

```python
import jax
import jax.numpy as jnp
from jax import lax
from jax.experimental import pallas as pl
from jax.experimental.pallas import tpu as pltpu
from jax.sharding import PartitionSpec as P

F32, BF16, I32 = jnp.float32, jnp.bfloat16, jnp.int32
MESH = pl.DeviceIdType.MESH
DEVS, CAP = 128, 12
SLOTS = DEVS * CAP
PAIRS, EMB, HID, IN = 512, 256, 512, 768
ROWS = 8192
UNITS, PIECE = 672, 7
UNITS_FIRST, UNITS_SECOND = 384, 256
VMEM_STEP = 50 << 20


def nt(a, b):
    return lax.dot_general(a, b, (((1,), (1,)), ((), ())), preferred_element_type=F32)


def tn(a, b):
    return lax.dot_general(a, b, (((0,), (0,)), ((), ())), preferred_element_type=F32)


def dot(a, b):
    return jnp.dot(a, b, preferred_element_type=F32)


def device(y, x, z, c):
    return ((y * 4 + x) * 4 + z) * 2 + c


def far_first(k):
    return 2 + k - 3 * (k // 2) - 2 * (k // 3)


ZC_ORDER = (4, 5, 2, 3, 6, 7, 1, 0)


def remote(src, dst, send, recv, to):
    return pltpu.make_async_remote_copy(
        src_ref=src, dst_ref=dst, send_sem=send, recv_sem=recv, device_id=(to,), device_id_type=MESH
    )


def step_kernel(
    owners, rows, labels, table, w_first, bias_first, w_second, bias_second, w_head, head_bias,
    tab32, gathered,
    incoming, row_ids, hot_rows, tab16, w1, w2,
    ask_send, ask_mid, ask_mid2, ask_got, ask_smem, slot_row, label_col,
    pick, place, stage, rows_send, rows_got, pack, fetched,
    feat, hid1, del1, del2, one_hot_grads, out32, grads_send,
    local32, local16, got_core, sum0, half0, got1, sum1, half1, got2, half2, got3,
    load_sem, ask1_s, ask1_r, ask2_s, ask2_r, smem_sem, row_s, row_r, grad_s, grad_r,
    core_s, core_r, rs1_s, rs1_r, rs2_s, rs2_r, x3_s, x3_r, ag2_s, ag2_r, ag1_s, ag1_r, agc_s, agc_r,
):
    me = lax.axis_index("dev")
    my, mx, mz, mc = me // 32, me // 8 % 4, me // 2 % 4, me % 2

    def zc_plus(j):
        return device(my, mx, (mz + j // 2) % 4, (mc + j) % 2)

    def yx_plus(i):
        return device((my + i // 4) % 4, (mx + i) % 4, mz, mc)

    def minus(i, j):
        return device((my + 4 - i // 4) % 4, (mx + 4 - i % 4) % 4, (mz + 4 - j // 2) % 4, (mc + j) % 2)

    def plus(i, j):
        return device((my + i // 4) % 4, (mx + i) % 4, (mz + j // 2) % 4, (mc + j) % 2)

    sent = []

    def flush():
        for wait in sent:
            wait()

    def start(copy):
        copy.start()
        sent.append(copy.wait_send)
        return copy

    barrier = pltpu.get_barrier_semaphore()
    for j in range(1, 8):
        pl.semaphore_signal(barrier, inc=1, device_id=(zc_plus(j),), device_id_type=MESH)
    for i in range(1, 16):
        pl.semaphore_signal(barrier, inc=1, device_id=(yx_plus(i),), device_id_type=MESH)

    loads = [
        pltpu.make_async_copy(
            table.at[pl.ds(k * 2048, 2048)], tab16.at[pl.ds(k * 2048, 2048)], load_sem.at[k]
        )
        for k in range(4)
    ] + [
        pltpu.make_async_copy(w_first, w1, load_sem.at[4]),
        pltpu.make_async_copy(w_second, w2, load_sem.at[5]),
    ]
    for load in loads:
        load.start()

    own = owners[...]
    d_y = ((own >> 5) - my) & 3
    d_x = ((own >> 3) - mx) & 3
    d_z = ((own >> 1) - mz) & 3
    d_c = (own - mc) & 1
    d_yx, d_zc = d_y * 4 + d_x, d_z * 2 + d_c
    ask_bucket, bucket = d_zc * 16 + d_yx, d_yx * 8 + d_zc
    row = rows[...]
    row_hi, row_lo = (row >> 6).astype(F32), (row & 63).astype(F32)
    sub = lax.broadcasted_iota(I32, (128, 128), 0)
    lane = lax.broadcasted_iota(I32, (128, 128), 1)
    earlier = jnp.where(sub < lane, 1.0, 0.0).astype(BF16)
    ones = jnp.ones((128, 128), BF16)
    in_lane = jnp.where(sub < 8 * CAP, sub % CAP, -1)

    def part(array, b):
        return array[b // 4 : b // 4 + 1, 128 * (b % 4) : 128 * (b % 4) + 128]

    hots32 = [jnp.where(sub == part(ask_bucket, b), 1.0, 0.0) for b in range(8)]
    hots = [hot.astype(BF16) for hot in hots32]
    counts = dot(jnp.concatenate(hots, axis=0), jnp.concatenate([earlier, ones], axis=1))
    carry = jnp.zeros((128, 128), F32)
    values = []
    for b in range(8):
        before = counts[128 * b : 128 * b + 128, :128] + carry
        carry = carry + counts[128 * b : 128 * b + 128, 128:]
        nth = jnp.sum(hots32[b] * before, axis=0, keepdims=True).astype(I32)
        hi = jnp.where(in_lane == nth, part(row_hi, b), 0.0).astype(BF16)
        lo = jnp.where(in_lane == nth, part(row_lo, b), 0.0).astype(BF16)
        values.append(jnp.concatenate([hi, lo], axis=0))
        slot_row[b] = part(bucket, b) * CAP + nth
    halves = nt(jnp.concatenate(hots, axis=1), jnp.concatenate(values, axis=1))
    ask = (halves[:, :128] * 64.0 + halves[:, 128:]).astype(I32)
    for j in range(8):
        ask_send[j] = ask[16 * j : 16 * j + 16]

    pl.semaphore_wait(barrier, 22)
    asks = []
    for j in range(1, 8):
        asks.append(start(remote(ask_send.at[j], ask_mid.at[j], ask1_s.at[j], ask1_r.at[j], zc_plus(j))))
    ask_mid[0] = ask_send[0]

    for k in range(4):
        loads[k].wait()

        @pl.loop(0, 32)
        def _(t):
            at = pl.ds(pl.multiple_of(k * 2048 + t * 64, 64), 64)
            tab32[at, :] = tab16[at, :].astype(F32)

    for copy in asks:
        copy.wait_recv()
    group = lax.broadcasted_iota(I32, (16, 128), 1) // CAP
    merged = ask_mid[0]
    for j in range(1, 8):
        merged = jnp.where(group == j, ask_mid[j], merged)
    for i in range(16):
        ask_mid2[i] = merged[i : i + 1]
    asks2 = []
    for i in range(1, 16):
        asks2.append(start(remote(ask_mid2.at[i], ask_got.at[i], ask2_s.at[i], ask2_r.at[i], yx_plus(i))))
    ask_got[0] = ask_mid2[0]

    for b in range(8):
        slot_b = slot_row[b]
        column = jnp.transpose(jnp.broadcast_to(slot_b.astype(F32), (128, 128))).astype(I32)

        @pl.loop(0, 12)
        def _(k):
            at = pl.ds(pl.multiple_of(k * 128, 128), 128)
            pick[128 * b : 128 * b + 128, at] = jnp.where(column == lane + k * 128, 1.0, 0.0).astype(BF16)
            place[at, 128 * b : 128 * b + 128] = jnp.where(sub + k * 128 == slot_b, 1.0, 0.0).astype(BF16)

    for b in range(4):
        part = labels[:, 128 * b : 128 * b + 128].astype(F32)
        label_col[128 * b : 128 * b + 128, :] = jnp.transpose(jnp.broadcast_to(part, (128, 128)))

    for copy in asks2:
        copy.wait_recv()
    to_smem = pltpu.make_async_copy(ask_got, ask_smem, smem_sem)
    to_smem.start()
    for i in range(16):
        row_ids[:, 8 * CAP * i : 8 * CAP * i + 8 * CAP] = ask_got[i][:, : 8 * CAP]
    to_smem.wait()

    def look_up(i, j, out):
        for c in range(CAP):
            asked = jnp.clip(ask_smem[i, 0, CAP * j + c], 0, ROWS - 1)
            stage[j, pl.ds(c, 1), :] = tab32[pl.ds(asked, 1), :]
        for q in range(3):
            out[q] = stage[j, 4 * q : 4 * q + 4, :].astype(BF16)

    def send_rows(i, j):
        r = i * 8 + j
        look_up(i, j, rows_send.at[r])
        remote(rows_send.at[r], rows_got.at[r], row_s, row_r, minus(i, j)).start()

    def rows_of(t, carry):
        i = far_first(t // 4) * 4 + far_first(t % 4)
        for j in ZC_ORDER:
            send_rows(i, j)
        return carry

    lax.fori_loop(0, 15, rows_of, 0)
    for j in ZC_ORDER[:-1]:
        send_rows(0, j)
    look_up(0, 0, rows_got.at[0])

    rest = pl.ds(1, DEVS - 1)
    sent.append(pltpu.make_async_copy(rows_send.at[rest], rows_send.at[rest], row_s).wait)
    for k in (4, 5):
        loads[k].wait()
    pltpu.make_async_copy(rows_got.at[rest], rows_got.at[rest], row_r).wait()

    def unpack(got):
        @pl.loop(0, 32)
        def _(g):
            for a in range(4):
                for q in range(3):
                    pack[12 * a + 4 * q : 12 * a + 4 * q + 4, :] = got[g * 4 + a, q].astype(F32)
            fetched[pl.ds(pl.multiple_of(g * 48, 16), 48), :] = pack[...].astype(BF16)

    unpack(rows_got)

    local32[...] = jnp.zeros_like(local32)
    head = w_head[...].reshape(1, HID).astype(F32)
    small = [jnp.zeros((1, HID), F32)] * 3
    for m in range(2):
        at = slice(256 * m, 256 * m + 256)
        first = dot(pick[256 * m : 256 * m + 256, :], fetched[...])
        second = dot(pick[PAIRS + 256 * m : PAIRS + 256 * m + 256, :], fetched[...])
        feat[at, 0:EMB] = first.astype(BF16)
        feat[at, EMB : 2 * EMB] = second.astype(BF16)
        feat[at, 2 * EMB :] = (first * second).astype(BF16)
        pre_first = dot(feat[at, :], w1[...]) + bias_first[...]
        hid1[at, :] = jnp.maximum(pre_first, 0.0).astype(BF16)
        pre_second = dot(hid1[at, :], w2[...]) + bias_second[...]
        hidden_second = jnp.maximum(pre_second, 0.0).astype(BF16).astype(F32)
        logit = jnp.sum(hidden_second * head, axis=1, keepdims=True) + head_bias[0]
        dlogit = 1.0 / (1.0 + jnp.exp(-logit)) - label_col[at, 0:1]
        delta_second = jnp.where(pre_second > 0, dlogit * head, 0.0).astype(BF16)
        del2[at, :] = delta_second
        delta_first = jnp.where(pre_first > 0, nt(delta_second, w2[...]), 0.0).astype(BF16)
        del1[at, :] = delta_first
        small = [
            small[0] + jnp.sum(delta_first.astype(F32), axis=0, keepdims=True),
            small[1] + jnp.sum(delta_second.astype(F32), axis=0, keepdims=True),
            small[2] + jnp.sum(hidden_second * dlogit, axis=0, keepdims=True),
        ]

    def put(unit, value):
        local32[unit] = value
        local16[unit] = value.astype(BF16)

    for block in range(3):
        grad = tn(feat[:, 256 * block : 256 * block + 256], del1[...])
        for t in range(32):
            for c in range(4):
                put(block * 128 + t * 4 + c, grad[8 * t : 8 * t + 8, 128 * c : 128 * c + 128])
    for block in range(2):
        grad = tn(hid1[:, 256 * block : 256 * block + 256], del2[...])
        for t in range(32):
            for c in range(4):
                put(
                    UNITS_FIRST + block * 128 + t * 4 + c,
                    grad[8 * t : 8 * t + 8, 128 * c : 128 * c + 128],
                )
    for c in range(4):
        for k in range(3):
            local32[640 + c, k : k + 1, :] = small[k][:, 128 * c : 128 * c + 128]
        local16[640 + c] = local32[640 + c].astype(BF16)
    for u in range(644, UNITS):
        local16[u] = jnp.zeros((8, 128), BF16)

    here = {"y": my, "x": mx, "z": mz}

    def along(axis, k):
        at = dict(here)
        at[axis] = (at[axis] + k) % 4
        return device(at["y"], at["x"], at["z"], mc)

    sibling = device(my, mx, mz, 1 - mc)
    lanes = (("y", "x", "z"), ("x", "z", "y"), ("z", "y", "x"))
    span1, span2 = 4 * PIECE, PIECE
    lane_units = 16 * PIECE

    def core_copy(l):
        at = pl.ds((1 - mc) * (UNITS // 2) + l * lane_units, lane_units)
        return remote(local16.at[at], got_core.at[l], core_s.at[l], core_r.at[l], sibling)

    def rs1_copy(l, k):
        axis = lanes[l][0]
        at = pl.ds((here[axis] + k) % 4 * span1, span1)
        return remote(half0.at[l, at], got1.at[l, k], rs1_s.at[l, k], rs1_r.at[l, k], along(axis, k))

    def rs2_copy(l, k):
        axis = lanes[l][1]
        at = pl.ds((here[axis] + k) % 4 * span2, span2)
        return remote(half1.at[l, at], got2.at[l, k], rs2_s.at[l, k], rs2_r.at[l, k], along(axis, k))

    def x3_copy(l, k):
        axis = lanes[l][2]
        return remote(half2.at[l], got3.at[l, here[axis]], x3_s.at[l, k], x3_r.at[l, k], along(axis, k))

    def unit_at(core, l, one, two=0):
        return core * (UNITS // 2) + l * lane_units + one * span1 + two * span2

    def ag2_copy(l, k):
        a, b = here[lanes[l][0]], here[lanes[l][1]]
        at = gathered.at[pl.ds(unit_at(mc, l, a, b), span2)]
        return remote(at, at, ag2_s.at[l, k], ag2_r.at[l, k], along(lanes[l][1], k))

    def ag1_copy(l, k):
        at = gathered.at[pl.ds(unit_at(mc, l, here[lanes[l][0]]), span1)]
        return remote(at, at, ag1_s.at[l, k], ag1_r.at[l, k], along(lanes[l][0], k))

    def agc_copy(l, k):
        at = gathered.at[pl.ds(unit_at(mc, l, (here[lanes[l][0]] + 4 - k) % 4), span1)]
        return remote(at, at, agc_s.at[l, k], agc_r.at[l, k], sibling)

    for l in range(3):
        start(core_copy(l))

    for m in range(2):
        at = slice(256 * m, 256 * m + 256)
        grad_input = nt(del1[at, :], w1[...])
        grad_product = grad_input[:, 2 * EMB :]
        grad_one = grad_input[:, :EMB] + grad_product * feat[at, EMB : 2 * EMB].astype(F32)
        grad_two = grad_input[:, EMB : 2 * EMB] + grad_product * feat[at, 0:EMB].astype(F32)
        one_hot_grads[256 * m : 256 * m + 256, :] = grad_one.astype(BF16)
        one_hot_grads[PAIRS + 256 * m : PAIRS + 256 * m + 256, :] = grad_two.astype(BF16)

    @pl.loop(0, 4)
    def _(k):
        at = pl.ds(pl.multiple_of(k * 384, 128), 384)
        out32[...] = dot(place[at, :], one_hot_grads[...])
        for r in range(32):
            for q in range(3):
                grads_send[k * 32 + r, q] = out32[12 * r + 4 * q : 12 * r + 4 * q + 4, :].astype(BF16)

    for l in range(3):
        core_copy(l).wait_recv()

        @pl.loop(0, 16)
        def _(t):
            at = pl.ds(t * PIECE, PIECE)
            total = (
                local32[pl.ds(mc * (UNITS // 2) + l * lane_units + t * PIECE, PIECE)]
                + got_core[l, at].astype(F32)
            )
            sum0[l, at] = total
            half0[l, at] = total.astype(BF16)

        for k in (2, 1, 3):
            start(rs1_copy(l, k))

    def grad_copy(i, j):
        r = i * 8 + j
        return remote(grads_send.at[r], incoming.at[r], grad_s, grad_r, plus(i, j))

    def grads_of(t, carry):
        i = far_first(t // 4) * 4 + far_first(t % 4)
        for j in ZC_ORDER:
            grad_copy(i, j).start()
        return carry

    lax.fori_loop(0, 15, grads_of, 0)
    for j in ZC_ORDER[:-1]:
        grad_copy(0, j).start()
    incoming[0] = grads_send[0]
    sent.append(pltpu.make_async_copy(grads_send.at[rest], grads_send.at[rest], grad_s).wait)

    for l in range(3):
        for k in range(1, 4):
            rs1_copy(l, k).wait_recv()
        for t in range(4):
            at = pl.ds(t * PIECE, PIECE)
            total = sum0[l, pl.ds(here[lanes[l][0]] * span1 + t * PIECE, PIECE)]
            for k in range(1, 4):
                total = total + got1[l, k, at].astype(F32)
            sum1[l, at] = total
            half1[l, at] = total.astype(BF16)
        for k in (2, 1, 3):
            start(rs2_copy(l, k))

    pltpu.make_async_copy(incoming.at[rest], incoming.at[rest], grad_r).wait()
    unpack(incoming)

    def update(quarter):
        for half in range(2):
            base = quarter * 2048 + half * 1024
            here_row = lax.broadcasted_iota(I32, (1024, SLOTS), 0) + base
            hot_rows[...] = jnp.where(here_row == row_ids[...], 1.0, 0.0).astype(BF16)
            at = slice(base, base + 1024)
            tab32[at, :] = tab32[at, :] - 8.0 * dot(hot_rows[...], fetched[...])

    update(0)
    for l in range(3):
        for k in range(1, 4):
            rs2_copy(l, k).wait_recv()
        total = sum1[l, pl.ds(here[lanes[l][1]] * span2, PIECE)]
        for k in range(1, 4):
            total = total + got2[l, k].astype(F32)
        half2[l] = total.astype(BF16)
        got3[l, here[lanes[l][2]]] = total.astype(BF16)
        for k in (2, 1, 3):
            start(x3_copy(l, k))
    update(1)
    for l in range(3):
        for k in range(1, 4):
            x3_copy(l, k).wait_recv()
        total = got3[l, 0].astype(F32)
        for a in range(1, 4):
            total = total + got3[l, a].astype(F32)
        gathered[pl.ds(unit_at(mc, l, here[lanes[l][0]], here[lanes[l][1]]), PIECE)] = total.astype(BF16)
        for k in (2, 1, 3):
            start(ag2_copy(l, k))
    update(2)
    for l in range(3):
        for k in range(1, 4):
            ag2_copy(l, k).wait_recv()
        for k in (2, 1, 3):
            start(ag1_copy(l, k))
        start(agc_copy(l, 0))
    update(3)
    for l in range(3):
        for k in (1, 3, 2):
            ag1_copy(l, k).wait_recv()
            start(agc_copy(l, k))
    for l in range(3):
        for k in range(4):
            agc_copy(l, k).wait_recv()

    flush()


def step(owners, rows, labels, table, w_first, bias_first, w_second, bias_second, w_head, head_bias):
    vmem = pl.BlockSpec(memory_space=pltpu.VMEM)
    any_ = pl.BlockSpec(memory_space=pl.ANY)
    dma = pltpu.SemaphoreType.DMA
    scratch = [
        pltpu.VMEM((DEVS, 3, 4, EMB), BF16),
        pltpu.VMEM((1, SLOTS), I32),
        pltpu.VMEM((1024, SLOTS), BF16),
        pltpu.VMEM((ROWS, EMB), BF16),
        pltpu.VMEM((IN, HID), BF16),
        pltpu.VMEM((HID, HID), BF16),
        pltpu.VMEM((8, 16, 128), I32),
        pltpu.VMEM((8, 16, 128), I32),
        pltpu.VMEM((16, 1, 128), I32),
        pltpu.VMEM((16, 1, 128), I32),
        pltpu.SMEM((16, 1, 128), I32),
        pltpu.VMEM((8, 1, 128), I32),
        pltpu.VMEM((PAIRS, 128), F32),
        pltpu.VMEM((2 * PAIRS, SLOTS), BF16),
        pltpu.VMEM((SLOTS, 2 * PAIRS), BF16),
        pltpu.VMEM((8, 16, EMB), F32),
        pltpu.VMEM((DEVS, 3, 4, EMB), BF16),
        pltpu.VMEM((DEVS, 3, 4, EMB), BF16),
        pltpu.VMEM((48, EMB), F32),
        pltpu.VMEM((SLOTS, EMB), BF16),
        pltpu.VMEM((PAIRS, IN), BF16),
        pltpu.VMEM((PAIRS, HID), BF16),
        pltpu.VMEM((PAIRS, HID), BF16),
        pltpu.VMEM((PAIRS, HID), BF16),
        pltpu.VMEM((2 * PAIRS, EMB), BF16),
        pltpu.VMEM((384, EMB), F32),
        pltpu.VMEM((DEVS, 3, 4, EMB), BF16),
        pltpu.VMEM((UNITS, 8, 128), F32),
        pltpu.VMEM((UNITS, 8, 128), BF16),
        pltpu.VMEM((3, 16 * PIECE, 8, 128), BF16),
        pltpu.VMEM((3, 16 * PIECE, 8, 128), F32),
        pltpu.VMEM((3, 16 * PIECE, 8, 128), BF16),
        pltpu.VMEM((3, 4, 4 * PIECE, 8, 128), BF16),
        pltpu.VMEM((3, 4 * PIECE, 8, 128), F32),
        pltpu.VMEM((3, 4 * PIECE, 8, 128), BF16),
        pltpu.VMEM((3, 4, PIECE, 8, 128), BF16),
        pltpu.VMEM((3, PIECE, 8, 128), BF16),
        pltpu.VMEM((3, 4, PIECE, 8, 128), BF16),
        dma((6,)), dma((8,)), dma((8,)), dma((16,)), dma((16,)), dma, dma, dma, dma, dma,
        dma((3,)), dma((3,)), dma((3, 4)), dma((3, 4)), dma((3, 4)), dma((3, 4)), dma((3, 4)), dma((3, 4)),
        dma((3, 4)), dma((3, 4)), dma((3, 4)), dma((3, 4)), dma((3, 4)), dma((3, 4)),
    ]
    return pl.pallas_call(
        step_kernel,
        out_shape=(pltpu.VMEM((ROWS, EMB), F32), pltpu.VMEM((UNITS, 8, 128), BF16)),
        in_specs=[vmem, vmem, vmem, any_, any_, vmem, any_, vmem, vmem, pl.BlockSpec(memory_space=pltpu.SMEM)],
        out_specs=(vmem, vmem),
        scratch_shapes=scratch,
        compiler_params=pltpu.CompilerParams(
            collective_id=0, has_side_effects=True, vmem_limit_bytes=VMEM_STEP
        ),
        name="exchange_and_mlp",
    )(owners, rows, labels, table, w_first, bias_first, w_second, bias_second, w_head, head_bias)


def finish_kernel(
    table, units, new_table, grad_first, grad_second, grad_small, first32, second32, table_sem, grad_sem
):
    parts = [
        pltpu.make_async_copy(
            table.at[pl.ds(k * 1024, 1024)], new_table.at[pl.ds(k * 1024, 1024)], table_sem.at[k]
        )
        for k in range(8)
    ]
    for part in parts:
        part.start()
    for array, out, first_unit in ((first32, grad_first, 0), (second32, grad_second, UNITS_FIRST)):

        @pl.loop(0, array.shape[0] // 32)
        def _(t):
            for u in range(4):
                at = pl.ds(pl.multiple_of(t * 32 + u * 8, 8), 8)
                for c in range(4):
                    array[at, 128 * c : 128 * c + 128] = units[first_unit + t * 16 + u * 4 + c].astype(F32)

        part = pltpu.make_async_copy(array, out, grad_sem.at[len(parts) - 8])
        part.start()
        parts.append(part)
    for c in range(4):
        grad_small[:, 128 * c : 128 * c + 128] = units[640 + c].astype(F32)[0:3]
    for part in parts:
        part.wait()


def finish(table, units):
    vmem = pl.BlockSpec(memory_space=pltpu.VMEM)
    any_ = pl.BlockSpec(memory_space=pl.ANY)
    return pl.pallas_call(
        finish_kernel,
        in_specs=[vmem, vmem],
        out_specs=(any_, any_, any_, vmem),
        out_shape=(
            jax.ShapeDtypeStruct((ROWS, EMB), F32),
            jax.ShapeDtypeStruct((IN, HID), F32),
            jax.ShapeDtypeStruct((HID, HID), F32),
            jax.ShapeDtypeStruct((3, HID), F32),
        ),
        scratch_shapes=[
            pltpu.VMEM((IN, HID), F32),
            pltpu.VMEM((HID, HID), F32),
            pltpu.SemaphoreType.DMA((8,)),
            pltpu.SemaphoreType.DMA((2,)),
        ],
        compiler_params=pltpu.CompilerParams(vmem_limit_bytes=8 << 20),
        name="write_out",
    )(pltpu.with_memory_space_constraint(table, pltpu.VMEM), pltpu.with_memory_space_constraint(units, pltpu.VMEM))


def on_device(
    node_table, owners, local_rows, labels, w_first, bias_first, w_second, bias_second, w_head, head_bias
):
    table, units = step(
        owners.T, local_rows.T, labels.reshape(1, PAIRS), node_table,
        w_first, bias_first.reshape(1, HID), w_second, bias_second.reshape(1, HID), w_head, head_bias,
    )
    return finish(table, units)


def solution(mesh):
    in_specs = (P("dev", None), P("dev", None), P("dev", None), P("dev"), P(), P(), P(), P(), P(), P())
    out_specs = (P("dev", None), P(), P(), P())
    return jax.shard_map(on_device, mesh=mesh, in_specs=in_specs, out_specs=out_specs, check_vma=False)
```

```python
import jax
import jax.numpy as jnp
from jax import lax
from jax.experimental import pallas as pl
from jax.experimental.pallas import tpu as pltpu
from jax.sharding import PartitionSpec as P

F32, BF16, I32 = jnp.float32, jnp.bfloat16, jnp.int32
MESH = pl.DeviceIdType.MESH
DEVS, CAP = 128, 12
SLOTS = DEVS * CAP
PAIRS, EMB, HID, IN = 512, 256, 512, 768
ROWS = 8192
UNITS, PIECE = 672, 7
UNITS_FIRST, UNITS_SECOND = 384, 256
VMEM_STEP = 50 << 20


def nt(a, b):
    return lax.dot_general(a, b, (((1,), (1,)), ((), ())), preferred_element_type=F32)


def tn(a, b):
    return lax.dot_general(a, b, (((0,), (0,)), ((), ())), preferred_element_type=F32)


def dot(a, b):
    return jnp.dot(a, b, preferred_element_type=F32)


def device(y, x, z, c):
    return ((y * 4 + x) * 4 + z) * 2 + c


FAR = ((2, 2), (2, 1), (2, 3), (1, 2), (3, 2), (1, 1), (3, 3), (1, 3), (3, 1), (2, 0), (0, 2), (1, 0), (3, 0), (0, 1), (0, 3), (0, 0))
ODD = tuple((y, x) for y, x in FAR if (y + x) % 2)
EVEN = tuple((y, x) for y, x in FAR if (y + x) % 2 == 0)
AG1_ORDER = ((2, 0), (2, 1), (1, 0), (3, 0), (1, 1), (3, 1), (0, 1))
ZC_ORDER = (4, 5, 2, 3, 6, 7, 1, 0)


def place_of(y, x):
    return (y + x) % 2 * 8 + y * 2 + x // 2


def remote(src, dst, send, recv, to):
    return pltpu.make_async_remote_copy(
        src_ref=src, dst_ref=dst, send_sem=send, recv_sem=recv, device_id=(to,), device_id_type=MESH
    )


def step_kernel(
    owners, rows, labels, table, w_first, bias_first, w_second, bias_second, w_head, head_bias,
    tab32, gathered,
    incoming, row_ids, hot_rows, tab16, w1, w2,
    ask_send, ask_mid, ask_mid2, ask_got, ask_smem, slot_row, label_col,
    pick, place, stage, rows_send, rows_got, pack, fetched,
    feat, hid1, del1, del2, one_hot_grads, out32, grads_send,
    local32, local16, got_core, sum0, half0, got1, sum1, half1, got2, half2, got3,
    load_sem, ask1_s, ask1_r, ask2_s, ask2_r, smem_sem, row_s, row_r, grad_s, grad_r,
    core_s, core_r, rs1_s, rs1_r, rs2_s, rs2_r, x3_s, x3_r, ag2_s, ag2_r, ag1_s, ag1_r,
):
    me = lax.axis_index("dev")
    my, mx, mz, mc = me // 32, me // 8 % 4, me // 2 % 4, me % 2

    def zc_plus(j):
        return device(my, mx, (mz + j // 2) % 4, (mc + j) % 2)

    def yx_plus(i):
        return device((my + i // 4) % 4, (mx + i) % 4, mz, mc)

    def minus(i, j):
        return device((my + 4 - i // 4) % 4, (mx + 4 - i % 4) % 4, (mz + 4 - j // 2) % 4, (mc + j) % 2)

    def plus(i, j):
        return device((my + i // 4) % 4, (mx + i) % 4, (mz + j // 2) % 4, (mc + j) % 2)

    sent = []

    def flush(waits):
        for wait in waits:
            wait()

    def start(copy):
        copy.start()
        sent.append(copy.wait_send)
        return copy

    barrier = pltpu.get_barrier_semaphore()
    for j in range(1, 8):
        pl.semaphore_signal(barrier, inc=1, device_id=(zc_plus(j),), device_id_type=MESH)
    for i in range(1, 16):
        pl.semaphore_signal(barrier, inc=1, device_id=(yx_plus(i),), device_id_type=MESH)

    loads = [
        pltpu.make_async_copy(
            table.at[pl.ds(k * 2048, 2048)], tab16.at[pl.ds(k * 2048, 2048)], load_sem.at[k]
        )
        for k in range(4)
    ] + [
        pltpu.make_async_copy(w_first, w1, load_sem.at[4]),
        pltpu.make_async_copy(w_second, w2, load_sem.at[5]),
    ]
    for load in loads:
        load.start()

    own = owners[...]
    d_y = ((own >> 5) - my) & 3
    d_x = ((own >> 3) - mx) & 3
    d_z = ((own >> 1) - mz) & 3
    d_c = (own - mc) & 1
    d_zc = d_z * 2 + d_c
    ask_bucket = d_zc * 16 + d_y * 4 + d_x
    bucket = (((d_y + d_x) & 1) * 8 + d_y * 2 + (d_x >> 1)) * 8 + d_zc
    row = rows[...]
    row_hi, row_lo = (row >> 6).astype(F32), (row & 63).astype(F32)
    sub = lax.broadcasted_iota(I32, (128, 128), 0)
    lane = lax.broadcasted_iota(I32, (128, 128), 1)
    earlier = jnp.where(sub < lane, 1.0, 0.0).astype(BF16)
    ones = jnp.ones((128, 128), BF16)
    in_lane = jnp.where(sub < 8 * CAP, sub % CAP, -1)

    def part(array, b):
        return array[b // 4 : b // 4 + 1, 128 * (b % 4) : 128 * (b % 4) + 128]

    hots32 = [jnp.where(sub == part(ask_bucket, b), 1.0, 0.0) for b in range(8)]
    hots = [hot.astype(BF16) for hot in hots32]
    counts = dot(jnp.concatenate(hots, axis=0), jnp.concatenate([earlier, ones], axis=1))
    carry = jnp.zeros((128, 128), F32)
    values = []
    for b in range(8):
        before = counts[128 * b : 128 * b + 128, :128] + carry
        carry = carry + counts[128 * b : 128 * b + 128, 128:]
        nth = jnp.sum(hots32[b] * before, axis=0, keepdims=True).astype(I32)
        hi = jnp.where(in_lane == nth, part(row_hi, b), 0.0).astype(BF16)
        lo = jnp.where(in_lane == nth, part(row_lo, b), 0.0).astype(BF16)
        values.append(jnp.concatenate([hi, lo], axis=0))
        slot_row[b] = part(bucket, b) * CAP + nth
    halves = nt(jnp.concatenate(hots, axis=1), jnp.concatenate(values, axis=1))
    ask = (halves[:, :128] * 64.0 + halves[:, 128:]).astype(I32)
    for j in range(8):
        ask_send[j] = ask[16 * j : 16 * j + 16]

    pl.semaphore_wait(barrier, 22)
    asks = []
    for j in range(1, 8):
        asks.append(start(remote(ask_send.at[j], ask_mid.at[j], ask1_s.at[j], ask1_r.at[j], zc_plus(j))))
    ask_mid[0] = ask_send[0]

    def widen(begin, end):
        for k in range(begin, end):
            loads[k].wait()

            @pl.loop(0, 16)
            def _(t):
                at = pl.ds(pl.multiple_of(k * 2048 + t * 128, 128), 128)
                tab32[at, :] = tab16[at, :].astype(F32)

    widen(0, 2)
    for copy in asks:
        copy.wait_recv()
    group = lax.broadcasted_iota(I32, (16, 128), 1) // CAP
    merged = ask_mid[0]
    for j in range(1, 8):
        merged = jnp.where(group == j, ask_mid[j], merged)
    for i in range(16):
        ask_mid2[i] = merged[i : i + 1]
    asks2 = []
    for i in range(1, 16):
        asks2.append(start(remote(ask_mid2.at[i], ask_got.at[i], ask2_s.at[i], ask2_r.at[i], yx_plus(i))))
    ask_got[0] = ask_mid2[0]

    widen(2, 4)
    for copy in asks2:
        copy.wait_recv()
    to_smem = pltpu.make_async_copy(ask_got, ask_smem, smem_sem)
    to_smem.start()
    for y, x in FAR:
        at = 8 * CAP * place_of(y, x)
        row_ids[:, at : at + 8 * CAP] = ask_got[y * 4 + x][:, : 8 * CAP]
    to_smem.wait()

    def look_up(i, j, out):
        for c in range(CAP):
            asked = jnp.clip(ask_smem[i, 0, CAP * j + c], 0, ROWS - 1)
            stage[j, pl.ds(c, 1), :] = tab32[pl.ds(asked, 1), :]
        for q in range(3):
            out[q] = stage[j, 4 * q : 4 * q + 4, :].astype(BF16)

    def send_rows(y, x, j):
        r = place_of(y, x) * 8 + j
        look_up(y * 4 + x, j, rows_send.at[r])
        remote(rows_send.at[r], rows_got.at[r], row_s, row_r, minus(y * 4 + x, j)).start()

    def column(_, digits):
        for j in ZC_ORDER:
            send_rows(digits % 16 // 4, digits % 4, j)
        return digits // 16

    for part in (FAR[:7], FAR[7:14]):
        lax.fori_loop(0, 7, column, sum((y * 4 + x) * 16**n for n, (y, x) in enumerate(part)))
    for j in ZC_ORDER:
        send_rows(*FAR[14], j)
    for j in ZC_ORDER[:-1]:
        send_rows(0, 0, j)
    look_up(0, 0, rows_got.at[0])

    for b in range(8):
        slot_b = slot_row[b]
        column = jnp.transpose(jnp.broadcast_to(slot_b.astype(F32), (128, 128))).astype(I32)

        @pl.loop(0, 12)
        def _(k):
            at = pl.ds(pl.multiple_of(k * 128, 128), 128)
            pick[128 * b : 128 * b + 128, at] = jnp.where(column == lane + k * 128, 1.0, 0.0).astype(BF16)
            place[at, 128 * b : 128 * b + 128] = jnp.where(sub + k * 128 == slot_b, 1.0, 0.0).astype(BF16)

    for b in range(4):
        part = labels[:, 128 * b : 128 * b + 128].astype(F32)
        label_col[128 * b : 128 * b + 128, :] = jnp.transpose(jnp.broadcast_to(part, (128, 128)))

    rest = pl.ds(1, DEVS - 1)
    sent.append(pltpu.make_async_copy(rows_send.at[rest], rows_send.at[rest], row_s).wait)
    for k in (4, 5):
        loads[k].wait()
    pltpu.make_async_copy(rows_got.at[rest], rows_got.at[rest], row_r).wait()

    def unpack(got, begin, end):
        @pl.loop(begin // 4, end // 4)
        def _(g):
            for a in range(4):
                for q in range(3):
                    pack[12 * a + 4 * q : 12 * a + 4 * q + 4, :] = got[g * 4 + a, q].astype(F32)
            fetched[pl.ds(pl.multiple_of(g * 48, 16), 48), :] = pack[...].astype(BF16)

    unpack(rows_got, 0, DEVS)

    local32[...] = jnp.zeros_like(local32)
    head = w_head[...].reshape(1, HID).astype(F32)
    small = [jnp.zeros((1, HID), F32)] * 3
    for m in range(2):
        at = slice(256 * m, 256 * m + 256)
        first = dot(pick[256 * m : 256 * m + 256, :], fetched[...])
        second = dot(pick[PAIRS + 256 * m : PAIRS + 256 * m + 256, :], fetched[...])
        feat[at, 0:EMB] = first.astype(BF16)
        feat[at, EMB : 2 * EMB] = second.astype(BF16)
        feat[at, 2 * EMB :] = (first * second).astype(BF16)
        pre_first = dot(feat[at, :], w1[...]) + bias_first[...]
        hid1[at, :] = jnp.maximum(pre_first, 0.0).astype(BF16)
        pre_second = dot(hid1[at, :], w2[...]) + bias_second[...]
        hidden_second = jnp.maximum(pre_second, 0.0).astype(BF16).astype(F32)
        logit = jnp.sum(hidden_second * head, axis=1, keepdims=True) + head_bias[0]
        dlogit = 1.0 / (1.0 + jnp.exp(-logit)) - label_col[at, 0:1]
        delta_second = jnp.where(pre_second > 0, dlogit * head, 0.0).astype(BF16)
        del2[at, :] = delta_second
        delta_first = jnp.where(pre_first > 0, nt(delta_second, w2[...]), 0.0).astype(BF16)
        del1[at, :] = delta_first
        small = [
            small[0] + jnp.sum(delta_first.astype(F32), axis=0, keepdims=True),
            small[1] + jnp.sum(delta_second.astype(F32), axis=0, keepdims=True),
            small[2] + jnp.sum(hidden_second * dlogit, axis=0, keepdims=True),
        ]

    for c in range(4):
        for k in range(3):
            local32[640 + c, k : k + 1, :] = small[k][:, 128 * c : 128 * c + 128]
        local16[640 + c] = local32[640 + c].astype(BF16)

    for m in range(2):
        at = slice(256 * m, 256 * m + 256)
        grad_input = nt(del1[at, :], w1[...])
        grad_product = grad_input[:, 2 * EMB :]
        grad_one = grad_input[:, :EMB] + grad_product * feat[at, EMB : 2 * EMB].astype(F32)
        grad_two = grad_input[:, EMB : 2 * EMB] + grad_product * feat[at, 0:EMB].astype(F32)
        one_hot_grads[256 * m : 256 * m + 256, :] = grad_one.astype(BF16)
        one_hot_grads[PAIRS + 256 * m : PAIRS + 256 * m + 256, :] = grad_two.astype(BF16)

    @pl.loop(0, 4)
    def _(k):
        at = pl.ds(pl.multiple_of(k * 384, 128), 384)
        out32[...] = dot(place[at, :], one_hot_grads[...])
        for r in range(32):
            for q in range(3):
                grads_send[k * 32 + r, q] = out32[12 * r + 4 * q : 12 * r + 4 * q + 4, :].astype(BF16)

    halves_at = (pl.ds(DEVS // 2, DEVS // 2), pl.ds(1, DEVS // 2 - 1))

    def send_grads(half, columns):
        for y, x in columns:
            for j in ZC_ORDER:
                r = place_of(y, x) * 8 + j
                if r:
                    copy = remote(
                        grads_send.at[r], incoming.at[r], grad_s.at[half], grad_r.at[half], plus(y * 4 + x, j)
                    )
                    copy.start()

    def sent_grads(half):
        at = grads_send.at[halves_at[half]]
        sent.append(pltpu.make_async_copy(at, at, grad_s.at[half]).wait)

    incoming[0] = grads_send[0]
    send_grads(0, ODD)
    sent_grads(0)
    def put(unit, value):
        local32[unit] = value
        local16[unit] = value.astype(BF16)

    for block in range(3):
        grad = tn(feat[:, 256 * block : 256 * block + 256], del1[...])
        for t in range(32):
            for c in range(4):
                put(block * 128 + t * 4 + c, grad[8 * t : 8 * t + 8, 128 * c : 128 * c + 128])
    for block in range(2):
        grad = tn(hid1[:, 256 * block : 256 * block + 256], del2[...])
        for t in range(32):
            for c in range(4):
                put(
                    UNITS_FIRST + block * 128 + t * 4 + c,
                    grad[8 * t : 8 * t + 8, 128 * c : 128 * c + 128],
                )
    for u in range(644, UNITS):
        local16[u] = jnp.zeros((8, 128), BF16)

    here = {"y": my, "x": mx, "z": mz}

    def along(axis, k, other=0):
        at = dict(here)
        at[axis] = (at[axis] + k) % 4
        return device(at["y"], at["x"], at["z"], (mc + other) % 2)

    sibling = device(my, mx, mz, 1 - mc)
    lanes = (("y", "x", "z"), ("x", "z", "y"), ("z", "y", "x"))
    span1, span2 = 4 * PIECE, PIECE
    lane_units = 16 * PIECE

    def core_copy(l):
        at = pl.ds((1 - mc) * (UNITS // 2) + l * lane_units, lane_units)
        return remote(local16.at[at], got_core.at[l], core_s.at[l], core_r.at[l], sibling)

    def rs1_copy(l, k):
        axis = lanes[l][0]
        at = pl.ds((here[axis] + k) % 4 * span1, span1)
        return remote(half0.at[l, at], got1.at[l, k], rs1_s.at[l, k], rs1_r.at[l, k], along(axis, k))

    def rs2_copy(l, k):
        axis = lanes[l][1]
        at = pl.ds((here[axis] + k) % 4 * span2, span2)
        return remote(half1.at[l, at], got2.at[l, k], rs2_s.at[l, k], rs2_r.at[l, k], along(axis, k))

    def x3_copy(l, k):
        axis = lanes[l][2]
        return remote(half2.at[l], got3.at[l, here[axis]], x3_s.at[l, k], x3_r.at[l, k], along(axis, k))

    def unit_at(core, l, one, two=0):
        return core * (UNITS // 2) + l * lane_units + one * span1 + two * span2

    def ag2_copy(l, k):
        a, b = here[lanes[l][0]], here[lanes[l][1]]
        at = gathered.at[pl.ds(unit_at(mc, l, a, b), span2)]
        return remote(at, at, ag2_s.at[l, k], ag2_r.at[l, k], along(lanes[l][1], k))

    def ag1_copy(l, k, other):
        at = gathered.at[pl.ds(unit_at(mc, l, here[lanes[l][0]]), span1)]
        to = along(lanes[l][0], k, other)
        return remote(at, at, ag1_s.at[l, k + 4 * other], ag1_r.at[l, k + 4 * other], to)

    for l in range(3):
        start(core_copy(l))

    def wait_grads(half):
        at = incoming.at[halves_at[half]]
        pltpu.make_async_copy(at, at, grad_r.at[half]).wait()
        unpack(incoming, DEVS // 2 * (1 - half), DEVS // 2 * (2 - half))

    def update(half, part):
        slots = slice(SLOTS // 2 * (1 - half), SLOTS // 2 * (2 - half))
        for block in range(4):
            base = part * 4096 + block * 1024
            here_row = lax.broadcasted_iota(I32, (1024, SLOTS // 2), 0) + base
            hot_rows[...] = jnp.where(here_row == row_ids[:, slots], 1.0, 0.0).astype(BF16)
            at = slice(base, base + 1024)
            tab32[at, :] = tab32[at, :] - 8.0 * dot(hot_rows[...], fetched[slots, :])

    for l in range(3):
        core_copy(l).wait_recv()

        @pl.loop(0, 16)
        def _(t):
            at = pl.ds(t * PIECE, PIECE)
            total = (
                local32[pl.ds(mc * (UNITS // 2) + l * lane_units + t * PIECE, PIECE)]
                + got_core[l, at].astype(F32)
            )
            sum0[l, at] = total
            half0[l, at] = total.astype(BF16)

        for k in (2, 1, 3):
            start(rs1_copy(l, k))

    for l in range(3):
        for k in range(1, 4):
            rs1_copy(l, k).wait_recv()
        for t in range(4):
            at = pl.ds(t * PIECE, PIECE)
            total = sum0[l, pl.ds(here[lanes[l][0]] * span1 + t * PIECE, PIECE)]
            for k in range(1, 4):
                total = total + got1[l, k, at].astype(F32)
            sum1[l, at] = total
            half1[l, at] = total.astype(BF16)
        for k in (2, 1, 3):
            start(rs2_copy(l, k))
    send_grads(1, EVEN[:3])

    wait_grads(0)
    update(0, 0)
    for l in range(3):
        for k in range(1, 4):
            rs2_copy(l, k).wait_recv()
        total = sum1[l, pl.ds(here[lanes[l][1]] * span2, PIECE)]
        for k in range(1, 4):
            total = total + got2[l, k].astype(F32)
        half2[l] = total.astype(BF16)
        got3[l, here[lanes[l][2]]] = total.astype(BF16)
        for k in (2, 1, 3):
            start(x3_copy(l, k))
    send_grads(1, EVEN[3:6])
    update(0, 1)
    for l in range(3):
        for k in range(1, 4):
            x3_copy(l, k).wait_recv()
        total = got3[l, 0].astype(F32)
        for a in range(1, 4):
            total = total + got3[l, a].astype(F32)
        gathered[pl.ds(unit_at(mc, l, here[lanes[l][0]], here[lanes[l][1]]), PIECE)] = total.astype(BF16)
        for k in (2, 1, 3):
            start(ag2_copy(l, k))
    send_grads(1, EVEN[6:])
    sent_grads(1)
    early, sent[:] = list(sent), []
    for l in range(3):
        for k in range(1, 4):
            ag2_copy(l, k).wait_recv()
        for k, other in AG1_ORDER:
            start(ag1_copy(l, k, other))
    flush(early)
    wait_grads(1)
    update(1, 0)
    update(1, 1)
    for l in range(3):
        for k, other in AG1_ORDER:
            ag1_copy(l, k, other).wait_recv()

    flush(sent)


def step(owners, rows, labels, table, w_first, bias_first, w_second, bias_second, w_head, head_bias):
    vmem = pl.BlockSpec(memory_space=pltpu.VMEM)
    any_ = pl.BlockSpec(memory_space=pl.ANY)
    dma = pltpu.SemaphoreType.DMA
    scratch = [
        pltpu.VMEM((DEVS, 3, 4, EMB), BF16),
        pltpu.VMEM((1, SLOTS), I32),
        pltpu.VMEM((1024, SLOTS // 2), BF16),
        pltpu.VMEM((ROWS, EMB), BF16),
        pltpu.VMEM((IN, HID), BF16),
        pltpu.VMEM((HID, HID), BF16),
        pltpu.VMEM((8, 16, 128), I32),
        pltpu.VMEM((8, 16, 128), I32),
        pltpu.VMEM((16, 1, 128), I32),
        pltpu.VMEM((16, 1, 128), I32),
        pltpu.SMEM((16, 1, 128), I32),
        pltpu.VMEM((8, 1, 128), I32),
        pltpu.VMEM((PAIRS, 128), F32),
        pltpu.VMEM((2 * PAIRS, SLOTS), BF16),
        pltpu.VMEM((SLOTS, 2 * PAIRS), BF16),
        pltpu.VMEM((8, 16, EMB), F32),
        pltpu.VMEM((DEVS, 3, 4, EMB), BF16),
        pltpu.VMEM((DEVS, 3, 4, EMB), BF16),
        pltpu.VMEM((48, EMB), F32),
        pltpu.VMEM((SLOTS, EMB), BF16),
        pltpu.VMEM((PAIRS, IN), BF16),
        pltpu.VMEM((PAIRS, HID), BF16),
        pltpu.VMEM((PAIRS, HID), BF16),
        pltpu.VMEM((PAIRS, HID), BF16),
        pltpu.VMEM((2 * PAIRS, EMB), BF16),
        pltpu.VMEM((384, EMB), F32),
        pltpu.VMEM((DEVS, 3, 4, EMB), BF16),
        pltpu.VMEM((UNITS, 8, 128), F32),
        pltpu.VMEM((UNITS, 8, 128), BF16),
        pltpu.VMEM((3, 16 * PIECE, 8, 128), BF16),
        pltpu.VMEM((3, 16 * PIECE, 8, 128), F32),
        pltpu.VMEM((3, 16 * PIECE, 8, 128), BF16),
        pltpu.VMEM((3, 4, 4 * PIECE, 8, 128), BF16),
        pltpu.VMEM((3, 4 * PIECE, 8, 128), F32),
        pltpu.VMEM((3, 4 * PIECE, 8, 128), BF16),
        pltpu.VMEM((3, 4, PIECE, 8, 128), BF16),
        pltpu.VMEM((3, PIECE, 8, 128), BF16),
        pltpu.VMEM((3, 4, PIECE, 8, 128), BF16),
        dma((6,)), dma((8,)), dma((8,)), dma((16,)), dma((16,)), dma, dma, dma, dma((2,)), dma((2,)),
        dma((3,)), dma((3,)), dma((3, 4)), dma((3, 4)), dma((3, 4)), dma((3, 4)), dma((3, 4)), dma((3, 4)),
        dma((3, 4)), dma((3, 4)), dma((3, 8)), dma((3, 8)),
    ]
    return pl.pallas_call(
        step_kernel,
        out_shape=(pltpu.VMEM((ROWS, EMB), F32), pltpu.VMEM((UNITS, 8, 128), BF16)),
        in_specs=[vmem, vmem, vmem, any_, any_, vmem, any_, vmem, vmem, pl.BlockSpec(memory_space=pltpu.SMEM)],
        out_specs=(vmem, vmem),
        scratch_shapes=scratch,
        compiler_params=pltpu.CompilerParams(
            collective_id=0, has_side_effects=True, vmem_limit_bytes=VMEM_STEP
        ),
        name="exchange_and_mlp",
    )(owners, rows, labels, table, w_first, bias_first, w_second, bias_second, w_head, head_bias)


def finish_kernel(
    table, units, new_table, grad_first, grad_second, grad_small, first32, second32, table_sem, grad_sem
):
    parts = [
        pltpu.make_async_copy(
            table.at[pl.ds(k * 1024, 1024)], new_table.at[pl.ds(k * 1024, 1024)], table_sem.at[k]
        )
        for k in range(8)
    ]
    for part in parts:
        part.start()
    for array, out, first_unit in ((first32, grad_first, 0), (second32, grad_second, UNITS_FIRST)):

        @pl.loop(0, array.shape[0] // 32)
        def _(t):
            for u in range(4):
                at = pl.ds(pl.multiple_of(t * 32 + u * 8, 8), 8)
                for c in range(4):
                    array[at, 128 * c : 128 * c + 128] = units[first_unit + t * 16 + u * 4 + c].astype(F32)

        part = pltpu.make_async_copy(array, out, grad_sem.at[len(parts) - 8])
        part.start()
        parts.append(part)
    for c in range(4):
        grad_small[:, 128 * c : 128 * c + 128] = units[640 + c].astype(F32)[0:3]
    for part in parts:
        part.wait()


def finish(table, units):
    vmem = pl.BlockSpec(memory_space=pltpu.VMEM)
    any_ = pl.BlockSpec(memory_space=pl.ANY)
    return pl.pallas_call(
        finish_kernel,
        in_specs=[vmem, vmem],
        out_specs=(any_, any_, any_, vmem),
        out_shape=(
            jax.ShapeDtypeStruct((ROWS, EMB), F32),
            jax.ShapeDtypeStruct((IN, HID), F32),
            jax.ShapeDtypeStruct((HID, HID), F32),
            jax.ShapeDtypeStruct((3, HID), F32),
        ),
        scratch_shapes=[
            pltpu.VMEM((IN, HID), F32),
            pltpu.VMEM((HID, HID), F32),
            pltpu.SemaphoreType.DMA((8,)),
            pltpu.SemaphoreType.DMA((2,)),
        ],
        compiler_params=pltpu.CompilerParams(vmem_limit_bytes=8 << 20),
        name="write_out",
    )(pltpu.with_memory_space_constraint(table, pltpu.VMEM), pltpu.with_memory_space_constraint(units, pltpu.VMEM))


def on_device(
    node_table, owners, local_rows, labels, w_first, bias_first, w_second, bias_second, w_head, head_bias
):
    table, units = step(
        owners.T, local_rows.T, labels.reshape(1, PAIRS), node_table,
        w_first, bias_first.reshape(1, HID), w_second, bias_second.reshape(1, HID), w_head, head_bias,
    )
    return finish(table, units)


def solution(mesh):
    in_specs = (P("dev", None), P("dev", None), P("dev", None), P("dev"), P(), P(), P(), P(), P(), P())
    out_specs = (P("dev", None), P(), P(), P())
    return jax.shard_map(on_device, mesh=mesh, in_specs=in_specs, out_specs=out_specs, check_vma=False)
```

```python
import jax
import jax.numpy as jnp
from jax import lax
from jax.experimental import pallas as pl
from jax.experimental.pallas import tpu as pltpu
from jax.sharding import PartitionSpec as P

F32, BF16, I32 = jnp.float32, jnp.bfloat16, jnp.int32
MESH = pl.DeviceIdType.MESH
DEVS, CAP = 128, 12
SLOTS = DEVS * CAP
PAIRS, EMB, HID, IN = 512, 256, 512, 768
ROWS = 8192
UNITS, PIECE = 672, 7
UNITS_FIRST, UNITS_SECOND = 384, 256
VMEM_STEP = 50 << 20


def nt(a, b):
    return lax.dot_general(a, b, (((1,), (1,)), ((), ())), preferred_element_type=F32)


def tn(a, b):
    return lax.dot_general(a, b, (((0,), (0,)), ((), ())), preferred_element_type=F32)


def dot(a, b):
    return jnp.dot(a, b, preferred_element_type=F32)


def device(y, x, z, c):
    return ((y * 4 + x) * 4 + z) * 2 + c


FAR = ((2, 2), (2, 1), (2, 3), (1, 2), (3, 2), (1, 1), (3, 3), (1, 3), (3, 1), (2, 0), (0, 2), (1, 0), (3, 0), (0, 1), (0, 3), (0, 0))
ODD = tuple((y, x) for y, x in FAR if (y + x) % 2)
EVEN = tuple((y, x) for y, x in FAR if (y + x) % 2 == 0)
AG1_ORDER = ((2, 0), (2, 1), (1, 0), (3, 0), (1, 1), (3, 1), (0, 1))
ZC_ORDER = (4, 5, 2, 3, 6, 7, 1, 0)


def unit_place(v):
    return v % 224 // 112 * (UNITS // 2) + v // 224 * 112 + v % 112


def place_of(y, x):
    return (y + x) % 2 * 8 + y * 2 + x // 2


def remote(src, dst, send, recv, to):
    return pltpu.make_async_remote_copy(
        src_ref=src, dst_ref=dst, send_sem=send, recv_sem=recv, device_id=(to,), device_id_type=MESH
    )


def step_kernel(
    owners, rows, labels, table, w_first, bias_first, w_second, bias_second, w_head, head_bias,
    tab32, gathered,
    incoming, row_ids, hot_rows, tab16, w1, w2,
    ask_send, ask_mid, ask_mid2, ask_got, ask_smem, slot_row, label_col,
    pick, picked, place, stage, rows_send, rows_got, pack, fetched,
    feat, hid1, del1, del2, one_hot_grads, out32, grads_send,
    local32, local16, got_core, sum0, half0, got1, sum1, half1, got2, half2, got3,
    load_sem, ask1_s, ask1_r, ask2_s, ask2_r, smem_sem, row_s, row_r, grad_s, grad_r,
    core_s, core_r, rs1_s, rs1_r, rs2_s, rs2_r, x3_s, x3_r, ag2_s, ag2_r, ag1_s, ag1_r,
):
    me = lax.axis_index("dev")
    my, mx, mz, mc = me // 32, me // 8 % 4, me // 2 % 4, me % 2

    def zc_plus(j):
        return device(my, mx, (mz + j // 2) % 4, (mc + j) % 2)

    def yx_plus(i):
        return device((my + i // 4) % 4, (mx + i) % 4, mz, mc)

    def minus(i, j):
        return device((my + 4 - i // 4) % 4, (mx + 4 - i % 4) % 4, (mz + 4 - j // 2) % 4, (mc + j) % 2)

    def plus(i, j):
        return device((my + i // 4) % 4, (mx + i) % 4, (mz + j // 2) % 4, (mc + j) % 2)

    sent = []

    def flush(waits):
        for wait in waits:
            wait()

    def start(copy):
        copy.start()
        sent.append(copy.wait_send)
        return copy

    barrier = pltpu.get_barrier_semaphore()
    for j in range(1, 8):
        pl.semaphore_signal(barrier, inc=1, device_id=(zc_plus(j),), device_id_type=MESH)
    for i in range(1, 16):
        pl.semaphore_signal(barrier, inc=1, device_id=(yx_plus(i),), device_id_type=MESH)

    loads = [
        pltpu.make_async_copy(
            table.at[pl.ds(k * 2048, 2048)], tab16.at[pl.ds(k * 2048, 2048)], load_sem.at[k]
        )
        for k in range(4)
    ] + [
        pltpu.make_async_copy(w_first, w1, load_sem.at[4]),
        pltpu.make_async_copy(w_second, w2, load_sem.at[5]),
    ]
    for load in loads:
        load.start()

    own = owners[...]
    d_y = ((own >> 5) - my) & 3
    d_x = ((own >> 3) - mx) & 3
    d_z = ((own >> 1) - mz) & 3
    d_c = (own - mc) & 1
    d_zc = d_z * 2 + d_c
    ask_bucket = d_zc * 16 + d_y * 4 + d_x
    bucket = (((d_y + d_x) & 1) * 8 + d_y * 2 + (d_x >> 1)) * 8 + d_zc
    row = rows[...]
    row_hi, row_lo = (row >> 6).astype(F32), (row & 63).astype(F32)
    sub = lax.broadcasted_iota(I32, (128, 128), 0)
    lane = lax.broadcasted_iota(I32, (128, 128), 1)
    earlier = jnp.where(sub < lane, 1.0, 0.0).astype(BF16)
    ones = jnp.ones((128, 128), BF16)
    in_lane = jnp.where(sub < 8 * CAP, sub % CAP, -1)

    def part(array, b):
        return array[b // 4 : b // 4 + 1, 128 * (b % 4) : 128 * (b % 4) + 128]

    hots32 = [jnp.where(sub == part(ask_bucket, b), 1.0, 0.0) for b in range(8)]
    hots = [hot.astype(BF16) for hot in hots32]
    counts = dot(jnp.concatenate(hots, axis=0), jnp.concatenate([earlier, ones], axis=1))
    carry = jnp.zeros((128, 128), F32)
    values = []
    for b in range(8):
        before = counts[128 * b : 128 * b + 128, :128] + carry
        carry = carry + counts[128 * b : 128 * b + 128, 128:]
        nth = jnp.sum(hots32[b] * before, axis=0, keepdims=True).astype(I32)
        hi = jnp.where(in_lane == nth, part(row_hi, b), 0.0).astype(BF16)
        lo = jnp.where(in_lane == nth, part(row_lo, b), 0.0).astype(BF16)
        values.append(jnp.concatenate([hi, lo], axis=0))
        slot_row[b] = part(bucket, b) * CAP + nth
    halves = nt(jnp.concatenate(hots, axis=1), jnp.concatenate(values, axis=1))
    ask = (halves[:, :128] * 64.0 + halves[:, 128:]).astype(I32)
    for j in range(8):
        ask_send[j] = ask[16 * j : 16 * j + 16]

    pl.semaphore_wait(barrier, 22)
    asks = []
    for j in range(1, 8):
        asks.append(start(remote(ask_send.at[j], ask_mid.at[j], ask1_s.at[j], ask1_r.at[j], zc_plus(j))))
    ask_mid[0] = ask_send[0]

    def widen(begin, end):
        for k in range(begin, end):
            loads[k].wait()

            @pl.loop(0, 16)
            def _(t):
                at = pl.ds(pl.multiple_of(k * 2048 + t * 128, 128), 128)
                tab32[at, :] = tab16[at, :].astype(F32)

    widen(0, 2)
    for copy in asks:
        copy.wait_recv()
    group = lax.broadcasted_iota(I32, (16, 128), 1) // CAP
    merged = ask_mid[0]
    for j in range(1, 8):
        merged = jnp.where(group == j, ask_mid[j], merged)
    for i in range(16):
        ask_mid2[i] = merged[i : i + 1]
    asks2 = []
    for i in range(1, 16):
        asks2.append(start(remote(ask_mid2.at[i], ask_got.at[i], ask2_s.at[i], ask2_r.at[i], yx_plus(i))))
    ask_got[0] = ask_mid2[0]

    widen(2, 4)
    for copy in asks2:
        copy.wait_recv()
    to_smem = pltpu.make_async_copy(ask_got, ask_smem, smem_sem)
    to_smem.start()
    for y, x in FAR:
        at = 8 * CAP * place_of(y, x)
        row_ids[:, at : at + 8 * CAP] = ask_got[y * 4 + x][:, : 8 * CAP]
    to_smem.wait()

    def look_up(i, j, out):
        for c in range(CAP):
            asked = jnp.clip(ask_smem[i, 0, CAP * j + c], 0, ROWS - 1)
            stage[j, pl.ds(c, 1), :] = tab32[pl.ds(asked, 1), :]
        for q in range(3):
            out[q] = stage[j, 4 * q : 4 * q + 4, :].astype(BF16)

    def send_rows(y, x, j):
        r = place_of(y, x) * 8 + j
        look_up(y * 4 + x, j, rows_send.at[r])
        half = 1 - (y + x) % 2
        remote(rows_send.at[r], rows_got.at[r], row_s, row_r.at[half], minus(y * 4 + x, j)).start()

    def column(_, digits):
        for j in ZC_ORDER:
            send_rows(digits % 16 // 4, digits % 4, j)
        return digits // 16

    columns = ODD + EVEN[:-1]
    for part in (columns[:7], columns[7:14]):
        lax.fori_loop(0, 7, column, sum((y * 4 + x) * 16**n for n, (y, x) in enumerate(part)))
    for j in ZC_ORDER:
        send_rows(*columns[14], j)
    for j in ZC_ORDER[:-1]:
        send_rows(0, 0, j)
    look_up(0, 0, rows_got.at[0])

    for b in range(8):
        slot_b = slot_row[b]
        column = jnp.transpose(jnp.broadcast_to(slot_b.astype(F32), (128, 128))).astype(I32)

        @pl.loop(0, 12)
        def _(k):
            at = pl.ds(pl.multiple_of(k * 128, 128), 128)
            pick[128 * b : 128 * b + 128, at] = jnp.where(column == lane + k * 128, 1.0, 0.0).astype(BF16)
            place[at, 128 * b : 128 * b + 128] = jnp.where(sub + k * 128 == slot_b, 1.0, 0.0).astype(BF16)

    for b in range(4):
        part = labels[:, 128 * b : 128 * b + 128].astype(F32)
        label_col[128 * b : 128 * b + 128, :] = jnp.transpose(jnp.broadcast_to(part, (128, 128)))

    rest = pl.ds(1, DEVS - 1)
    sent.append(pltpu.make_async_copy(rows_send.at[rest], rows_send.at[rest], row_s).wait)
    for k in (4, 5):
        loads[k].wait()
    def unpack(got, begin, end):
        @pl.loop(begin // 4, end // 4)
        def _(g):
            for a in range(4):
                for q in range(3):
                    pack[12 * a + 4 * q : 12 * a + 4 * q + 4, :] = got[g * 4 + a, q].astype(F32)
            fetched[pl.ds(pl.multiple_of(g * 48, 16), 48), :] = pack[...].astype(BF16)

    def wait_rows(half):
        at = rows_got.at[halves_at[half]]
        pltpu.make_async_copy(at, at, row_r.at[half]).wait()
        unpack(rows_got, DEVS // 2 * (1 - half), DEVS // 2 * (2 - half))

    halves_at = (pl.ds(DEVS // 2, DEVS // 2), pl.ds(1, DEVS // 2 - 1))
    lower, upper = slice(0, SLOTS // 2), slice(SLOTS // 2, SLOTS)
    wait_rows(0)
    picked[...] = dot(pick[:, upper], fetched[upper, :])
    wait_rows(1)

    local32[...] = jnp.zeros_like(local32)
    head = w_head[...].reshape(1, HID).astype(F32)
    small = [jnp.zeros((1, HID), F32)] * 3
    for m in range(2):
        at = slice(256 * m, 256 * m + 256)
        at2 = slice(PAIRS + 256 * m, PAIRS + 256 * m + 256)
        first = picked[at, :] + dot(pick[at, lower], fetched[lower, :])
        second = picked[at2, :] + dot(pick[at2, lower], fetched[lower, :])
        feat[at, 0:EMB] = first.astype(BF16)
        feat[at, EMB : 2 * EMB] = second.astype(BF16)
        feat[at, 2 * EMB :] = (first * second).astype(BF16)
        pre_first = dot(feat[at, :], w1[...]) + bias_first[...]
        hid1[at, :] = jnp.maximum(pre_first, 0.0).astype(BF16)
        pre_second = dot(hid1[at, :], w2[...]) + bias_second[...]
        hidden_second = jnp.maximum(pre_second, 0.0).astype(BF16).astype(F32)
        logit = jnp.sum(hidden_second * head, axis=1, keepdims=True) + head_bias[0]
        dlogit = 1.0 / (1.0 + jnp.exp(-logit)) - label_col[at, 0:1]
        delta_second = jnp.where(pre_second > 0, dlogit * head, 0.0).astype(BF16)
        del2[at, :] = delta_second
        delta_first = jnp.where(pre_first > 0, nt(delta_second, w2[...]), 0.0).astype(BF16)
        del1[at, :] = delta_first
        small = [
            small[0] + jnp.sum(delta_first.astype(F32), axis=0, keepdims=True),
            small[1] + jnp.sum(delta_second.astype(F32), axis=0, keepdims=True),
            small[2] + jnp.sum(hidden_second * dlogit, axis=0, keepdims=True),
        ]

    for c in range(4):
        for k in range(3):
            local32[unit_place(640 + c), k : k + 1, :] = small[k][:, 128 * c : 128 * c + 128]
        local16[unit_place(640 + c)] = local32[unit_place(640 + c)].astype(BF16)

    here = {"y": my, "x": mx, "z": mz}

    def along(axis, k, other=0):
        at = dict(here)
        at[axis] = (at[axis] + k) % 4
        return device(at["y"], at["x"], at["z"], (mc + other) % 2)

    sibling = device(my, mx, mz, 1 - mc)
    lanes = (("y", "x", "z"), ("x", "z", "y"), ("z", "y", "x"))
    span1, span2 = 4 * PIECE, PIECE
    lane_units = 16 * PIECE

    def core_copy(l):
        at = pl.ds((1 - mc) * (UNITS // 2) + l * lane_units, lane_units)
        return remote(local16.at[at], got_core.at[l], core_s.at[l], core_r.at[l], sibling)

    def rs1_copy(l, k):
        axis = lanes[l][0]
        at = pl.ds((here[axis] + k) % 4 * span1, span1)
        return remote(half0.at[l, at], got1.at[l, k], rs1_s.at[l, k], rs1_r.at[l, k], along(axis, k))

    def rs2_copy(l, k):
        axis = lanes[l][1]
        at = pl.ds((here[axis] + k) % 4 * span2, span2)
        return remote(half1.at[l, at], got2.at[l, k], rs2_s.at[l, k], rs2_r.at[l, k], along(axis, k))

    def x3_copy(l, k):
        axis = lanes[l][2]
        return remote(half2.at[l], got3.at[l, here[axis]], x3_s.at[l, k], x3_r.at[l, k], along(axis, k))

    def unit_at(core, l, one, two=0):
        return core * (UNITS // 2) + l * lane_units + one * span1 + two * span2

    def ag2_copy(l, k):
        a, b = here[lanes[l][0]], here[lanes[l][1]]
        at = gathered.at[pl.ds(unit_at(mc, l, a, b), span2)]
        return remote(at, at, ag2_s.at[l, k], ag2_r.at[l, k], along(lanes[l][1], k))

    def ag1_copy(l, k, other):
        at = gathered.at[pl.ds(unit_at(mc, l, here[lanes[l][0]]), span1)]
        to = along(lanes[l][0], k, other)
        return remote(at, at, ag1_s.at[l, k + 4 * other], ag1_r.at[l, k + 4 * other], to)

    def put(v, value):
        unit = unit_place(v)
        local32[unit] = value
        local16[unit] = value.astype(BF16)

    def put_block(first, grad):
        for n in range(32):
            for c in range(4):
                put(first + n * 4 + c, grad[8 * n : 8 * n + 8, 128 * c : 128 * c + 128])

    for u in range(644, UNITS):
        local16[unit_place(u)] = jnp.zeros((8, 128), BF16)
    for block in range(3):
        put_block(block * 128, tn(feat[:, 256 * block : 256 * block + 256], del1[...]))
        if block == 1:
            start(core_copy(0))
    for block in range(2):
        put_block(UNITS_FIRST + block * 128, tn(hid1[:, 256 * block : 256 * block + 256], del2[...]))
        start(core_copy(1 + block))


    for m in range(2):
        at = slice(256 * m, 256 * m + 256)
        grad_input = nt(del1[at, :], w1[...])
        grad_product = grad_input[:, 2 * EMB :]
        grad_one = grad_input[:, :EMB] + grad_product * feat[at, EMB : 2 * EMB].astype(F32)
        grad_two = grad_input[:, EMB : 2 * EMB] + grad_product * feat[at, 0:EMB].astype(F32)
        one_hot_grads[256 * m : 256 * m + 256, :] = grad_one.astype(BF16)
        one_hot_grads[PAIRS + 256 * m : PAIRS + 256 * m + 256, :] = grad_two.astype(BF16)

    @pl.loop(0, 4)
    def _(k):
        at = pl.ds(pl.multiple_of(k * 384, 128), 384)
        out32[...] = dot(place[at, :], one_hot_grads[...])
        for r in range(32):
            for q in range(3):
                grads_send[k * 32 + r, q] = out32[12 * r + 4 * q : 12 * r + 4 * q + 4, :].astype(BF16)

    def send_grads(half, columns):
        for y, x in columns:
            for j in ZC_ORDER:
                r = place_of(y, x) * 8 + j
                if r:
                    copy = remote(
                        grads_send.at[r], incoming.at[r], grad_s.at[half], grad_r.at[half], plus(y * 4 + x, j)
                    )
                    copy.start()

    def sent_grads(half):
        at = grads_send.at[halves_at[half]]
        sent.append(pltpu.make_async_copy(at, at, grad_s.at[half]).wait)

    incoming[0] = grads_send[0]
    def wait_grads(half):
        at = incoming.at[halves_at[half]]
        pltpu.make_async_copy(at, at, grad_r.at[half]).wait()
        unpack(incoming, DEVS // 2 * (1 - half), DEVS // 2 * (2 - half))

    def update(half, begin, end):
        slots = slice(SLOTS // 2 * (1 - half), SLOTS // 2 * (2 - half))
        for base in range(begin * 1024, end * 1024, 1024):
            here_row = lax.broadcasted_iota(I32, (1024, SLOTS // 2), 0) + base
            hot_rows[...] = jnp.where(here_row == row_ids[:, slots], 1.0, 0.0).astype(BF16)
            at = slice(base, base + 1024)
            tab32[at, :] = tab32[at, :] - 8.0 * dot(hot_rows[...], fetched[slots, :])

    send_grads(0, ODD)
    sent_grads(0)
    for l in range(3):
        core_copy(l).wait_recv()

        @pl.loop(0, 16)
        def _(t):
            at = pl.ds(t * PIECE, PIECE)
            total = (
                local32[pl.ds(mc * (UNITS // 2) + l * lane_units + t * PIECE, PIECE)]
                + got_core[l, at].astype(F32)
            )
            sum0[l, at] = total
            half0[l, at] = total.astype(BF16)

        for k in (2, 1, 3):
            start(rs1_copy(l, k))

    for l in range(3):
        for k in range(1, 4):
            rs1_copy(l, k).wait_recv()
        for t in range(4):
            at = pl.ds(t * PIECE, PIECE)
            total = sum0[l, pl.ds(here[lanes[l][0]] * span1 + t * PIECE, PIECE)]
            for k in range(1, 4):
                total = total + got1[l, k, at].astype(F32)
            sum1[l, at] = total
            half1[l, at] = total.astype(BF16)
        for k in (2, 1, 3):
            start(rs2_copy(l, k))
    send_grads(1, EVEN[:4])

    wait_grads(0)
    update(0, 0, 3)
    for l in range(3):
        for k in range(1, 4):
            rs2_copy(l, k).wait_recv()
        total = sum1[l, pl.ds(here[lanes[l][1]] * span2, PIECE)]
        for k in range(1, 4):
            total = total + got2[l, k].astype(F32)
        half2[l] = total.astype(BF16)
        got3[l, here[lanes[l][2]]] = total.astype(BF16)
        for k in (2, 1, 3):
            start(x3_copy(l, k))
    send_grads(1, EVEN[4:])
    update(0, 3, 6)
    for l in range(3):
        for k in range(1, 4):
            x3_copy(l, k).wait_recv()
        total = got3[l, 0].astype(F32)
        for a in range(1, 4):
            total = total + got3[l, a].astype(F32)
        gathered[pl.ds(unit_at(mc, l, here[lanes[l][0]], here[lanes[l][1]]), PIECE)] = total.astype(BF16)
        for k in (2, 1, 3):
            start(ag2_copy(l, k))
    sent_grads(1)
    early, sent[:] = list(sent), []
    update(0, 6, 8)
    for l in range(3):
        for k in range(1, 4):
            ag2_copy(l, k).wait_recv()
        for k, other in AG1_ORDER:
            start(ag1_copy(l, k, other))
    flush(early)
    wait_grads(1)
    update(1, 0, 8)
    for l in range(3):
        for k, other in AG1_ORDER:
            ag1_copy(l, k, other).wait_recv()

    flush(sent)


def step(owners, rows, labels, table, w_first, bias_first, w_second, bias_second, w_head, head_bias):
    vmem = pl.BlockSpec(memory_space=pltpu.VMEM)
    any_ = pl.BlockSpec(memory_space=pl.ANY)
    dma = pltpu.SemaphoreType.DMA
    scratch = [
        pltpu.VMEM((DEVS, 3, 4, EMB), BF16),
        pltpu.VMEM((1, SLOTS), I32),
        pltpu.VMEM((1024, SLOTS // 2), BF16),
        pltpu.VMEM((ROWS, EMB), BF16),
        pltpu.VMEM((IN, HID), BF16),
        pltpu.VMEM((HID, HID), BF16),
        pltpu.VMEM((8, 16, 128), I32),
        pltpu.VMEM((8, 16, 128), I32),
        pltpu.VMEM((16, 1, 128), I32),
        pltpu.VMEM((16, 1, 128), I32),
        pltpu.SMEM((16, 1, 128), I32),
        pltpu.VMEM((8, 1, 128), I32),
        pltpu.VMEM((PAIRS, 128), F32),
        pltpu.VMEM((2 * PAIRS, SLOTS), BF16),
        pltpu.VMEM((2 * PAIRS, EMB), F32),
        pltpu.VMEM((SLOTS, 2 * PAIRS), BF16),
        pltpu.VMEM((8, 16, EMB), F32),
        pltpu.VMEM((DEVS, 3, 4, EMB), BF16),
        pltpu.VMEM((DEVS, 3, 4, EMB), BF16),
        pltpu.VMEM((48, EMB), F32),
        pltpu.VMEM((SLOTS, EMB), BF16),
        pltpu.VMEM((PAIRS, IN), BF16),
        pltpu.VMEM((PAIRS, HID), BF16),
        pltpu.VMEM((PAIRS, HID), BF16),
        pltpu.VMEM((PAIRS, HID), BF16),
        pltpu.VMEM((2 * PAIRS, EMB), BF16),
        pltpu.VMEM((384, EMB), F32),
        pltpu.VMEM((DEVS, 3, 4, EMB), BF16),
        pltpu.VMEM((UNITS, 8, 128), F32),
        pltpu.VMEM((UNITS, 8, 128), BF16),
        pltpu.VMEM((3, 16 * PIECE, 8, 128), BF16),
        pltpu.VMEM((3, 16 * PIECE, 8, 128), F32),
        pltpu.VMEM((3, 16 * PIECE, 8, 128), BF16),
        pltpu.VMEM((3, 4, 4 * PIECE, 8, 128), BF16),
        pltpu.VMEM((3, 4 * PIECE, 8, 128), F32),
        pltpu.VMEM((3, 4 * PIECE, 8, 128), BF16),
        pltpu.VMEM((3, 4, PIECE, 8, 128), BF16),
        pltpu.VMEM((3, PIECE, 8, 128), BF16),
        pltpu.VMEM((3, 4, PIECE, 8, 128), BF16),
        dma((6,)), dma((8,)), dma((8,)), dma((16,)), dma((16,)), dma, dma, dma((2,)), dma((2,)), dma((2,)),
        dma((3,)), dma((3,)), dma((3, 4)), dma((3, 4)), dma((3, 4)), dma((3, 4)), dma((3, 4)), dma((3, 4)),
        dma((3, 4)), dma((3, 4)), dma((3, 8)), dma((3, 8)),
    ]
    return pl.pallas_call(
        step_kernel,
        out_shape=(pltpu.VMEM((ROWS, EMB), F32), pltpu.VMEM((UNITS, 8, 128), BF16)),
        in_specs=[vmem, vmem, vmem, any_, any_, vmem, any_, vmem, vmem, pl.BlockSpec(memory_space=pltpu.SMEM)],
        out_specs=(vmem, vmem),
        scratch_shapes=scratch,
        compiler_params=pltpu.CompilerParams(
            collective_id=0, has_side_effects=True, vmem_limit_bytes=VMEM_STEP
        ),
        name="exchange_and_mlp",
    )(owners, rows, labels, table, w_first, bias_first, w_second, bias_second, w_head, head_bias)


def finish_kernel(
    table, units, new_table, grad_first, grad_second, grad_small, first32, second32, table_sem, grad_sem
):
    parts = [
        pltpu.make_async_copy(
            table.at[pl.ds(k * 1024, 1024)], new_table.at[pl.ds(k * 1024, 1024)], table_sem.at[k]
        )
        for k in range(8)
    ]
    for part in parts:
        part.start()
    for array, out, first_unit in ((first32, grad_first, 0), (second32, grad_second, UNITS_FIRST)):

        @pl.loop(0, array.shape[0] // 32)
        def _(t):
            for u in range(4):
                at = pl.ds(pl.multiple_of(t * 32 + u * 8, 8), 8)
                for c in range(4):
                    array[at, 128 * c : 128 * c + 128] = units[unit_place(first_unit + t * 16) + u * 4 + c].astype(F32)

        part = pltpu.make_async_copy(array, out, grad_sem.at[len(parts) - 8])
        part.start()
        parts.append(part)
    for c in range(4):
        grad_small[:, 128 * c : 128 * c + 128] = units[unit_place(640 + c)].astype(F32)[0:3]
    for part in parts:
        part.wait()


def finish(table, units):
    vmem = pl.BlockSpec(memory_space=pltpu.VMEM)
    any_ = pl.BlockSpec(memory_space=pl.ANY)
    return pl.pallas_call(
        finish_kernel,
        in_specs=[vmem, vmem],
        out_specs=(any_, any_, any_, vmem),
        out_shape=(
            jax.ShapeDtypeStruct((ROWS, EMB), F32),
            jax.ShapeDtypeStruct((IN, HID), F32),
            jax.ShapeDtypeStruct((HID, HID), F32),
            jax.ShapeDtypeStruct((3, HID), F32),
        ),
        scratch_shapes=[
            pltpu.VMEM((IN, HID), F32),
            pltpu.VMEM((HID, HID), F32),
            pltpu.SemaphoreType.DMA((8,)),
            pltpu.SemaphoreType.DMA((2,)),
        ],
        compiler_params=pltpu.CompilerParams(vmem_limit_bytes=8 << 20),
        name="write_out",
    )(pltpu.with_memory_space_constraint(table, pltpu.VMEM), pltpu.with_memory_space_constraint(units, pltpu.VMEM))


def on_device(
    node_table, owners, local_rows, labels, w_first, bias_first, w_second, bias_second, w_head, head_bias
):
    table, units = step(
        owners.T, local_rows.T, labels.reshape(1, PAIRS), node_table,
        w_first, bias_first.reshape(1, HID), w_second, bias_second.reshape(1, HID), w_head, head_bias,
    )
    return finish(table, units)


def solution(mesh):
    in_specs = (P("dev", None), P("dev", None), P("dev", None), P("dev"), P(), P(), P(), P(), P(), P())
    out_specs = (P("dev", None), P(), P(), P())
    return jax.shard_map(on_device, mesh=mesh, in_specs=in_specs, out_specs=out_specs, check_vma=False)
```

```python
import jax
import jax.numpy as jnp
from jax import lax
from jax.experimental import pallas as pl
from jax.experimental.pallas import tpu as pltpu
from jax.sharding import PartitionSpec as P

F32, BF16, I32 = jnp.float32, jnp.bfloat16, jnp.int32
MESH = pl.DeviceIdType.MESH
DEVS, CAP = 128, 12
SLOTS = DEVS * CAP
PAIRS, EMB, HID, IN = 512, 256, 512, 768
ROWS = 8192
UNITS, PIECE = 672, 7
UNITS_FIRST, UNITS_SECOND = 384, 256
VMEM_STEP = 50 << 20


def nt(a, b):
    return lax.dot_general(a, b, (((1,), (1,)), ((), ())), preferred_element_type=F32)


def tn(a, b):
    return lax.dot_general(a, b, (((0,), (0,)), ((), ())), preferred_element_type=F32)


def dot(a, b):
    return jnp.dot(a, b, preferred_element_type=F32)


def device(y, x, z, c):
    return ((y * 4 + x) * 4 + z) * 2 + c


FAR = ((2, 2), (2, 1), (2, 3), (1, 2), (3, 2), (1, 1), (3, 3), (1, 3), (3, 1), (2, 0), (0, 2), (1, 0), (3, 0), (0, 1), (0, 3), (0, 0))
ODD = tuple((y, x) for y, x in FAR if (y + x) % 2)
EVEN = tuple((y, x) for y, x in FAR if (y + x) % 2 == 0)
AG1_ORDER = ((2, 0), (2, 1), (1, 0), (3, 0), (1, 1), (3, 1), (0, 1))
ZC_ORDER = (4, 5, 2, 3, 6, 7, 1, 0)


def unit_place(v):
    return v % 224 // 112 * (UNITS // 2) + v // 224 * 112 + v % 112


def place_of(y, x):
    return (y + x) % 2 * 8 + y * 2 + x // 2


def remote(src, dst, send, recv, to):
    return pltpu.make_async_remote_copy(
        src_ref=src, dst_ref=dst, send_sem=send, recv_sem=recv, device_id=(to,), device_id_type=MESH
    )


def step_kernel(
    owners, rows, labels, table, w_first, bias_first, w_second, bias_second, w_head, head_bias,
    tab32, gathered,
    incoming, row_ids, hot_rows, tab16, w1, w2,
    ask_send, ask_mid, ask_mid2, ask_got, ask_smem, slot_row, label_col,
    pick, picked, place, stage, rows_send, rows_got, pack, fetched,
    feat, hid1, del1, del2, one_hot_grads, out32, grads_send,
    local32, local16, got_core, sum0, half0, got1, sum1, half1, got2, half2, got3,
    load_sem, ask1_s, ask1_r, ask2_s, ask2_r, smem_sem, row_s, row_r, grad_s, grad_r,
    core_s, core_r, rs1_s, rs1_r, rs2_s, rs2_r, x3_s, x3_r, ag2_s, ag2_r, ag1_s, ag1_r,
):
    me = lax.axis_index("dev")
    my, mx, mz, mc = me // 32, me // 8 % 4, me // 2 % 4, me % 2

    def zc_plus(j):
        return device(my, mx, (mz + j // 2) % 4, (mc + j) % 2)

    def yx_plus(i):
        return device((my + i // 4) % 4, (mx + i) % 4, mz, mc)

    def minus(i, j):
        return device((my + 4 - i // 4) % 4, (mx + 4 - i % 4) % 4, (mz + 4 - j // 2) % 4, (mc + j) % 2)

    def plus(i, j):
        return device((my + i // 4) % 4, (mx + i) % 4, (mz + j // 2) % 4, (mc + j) % 2)

    sent = []

    def flush(waits):
        for wait in waits:
            wait()

    def start(copy):
        copy.start()
        sent.append(copy.wait_send)
        return copy

    barrier = pltpu.get_barrier_semaphore()
    for j in range(1, 8):
        pl.semaphore_signal(barrier, inc=1, device_id=(zc_plus(j),), device_id_type=MESH)
    for i in range(1, 16):
        pl.semaphore_signal(barrier, inc=1, device_id=(yx_plus(i),), device_id_type=MESH)

    loads = [
        pltpu.make_async_copy(
            table.at[pl.ds(k * 2048, 2048)], tab16.at[pl.ds(k * 2048, 2048)], load_sem.at[k]
        )
        for k in range(4)
    ] + [
        pltpu.make_async_copy(w_first, w1, load_sem.at[4]),
        pltpu.make_async_copy(w_second, w2, load_sem.at[5]),
    ]
    for load in loads:
        load.start()

    own = owners[...]
    d_y = ((own >> 5) - my) & 3
    d_x = ((own >> 3) - mx) & 3
    d_z = ((own >> 1) - mz) & 3
    d_c = (own - mc) & 1
    d_zc = d_z * 2 + d_c
    ask_bucket = d_zc * 16 + d_y * 4 + d_x
    bucket = (((d_y + d_x) & 1) * 8 + d_y * 2 + (d_x >> 1)) * 8 + d_zc
    row = rows[...]
    row_hi, row_lo = (row >> 6).astype(F32), (row & 63).astype(F32)
    sub = lax.broadcasted_iota(I32, (128, 128), 0)
    lane = lax.broadcasted_iota(I32, (128, 128), 1)
    earlier = jnp.where(sub < lane, 1.0, 0.0).astype(BF16)
    ones = jnp.ones((128, 128), BF16)
    in_lane = jnp.where(sub < 8 * CAP, sub % CAP, -1)

    def part(array, b):
        return array[b // 4 : b // 4 + 1, 128 * (b % 4) : 128 * (b % 4) + 128]

    hots32 = [jnp.where(sub == part(ask_bucket, b), 1.0, 0.0) for b in range(8)]
    hots = [hot.astype(BF16) for hot in hots32]
    counts = dot(jnp.concatenate(hots, axis=0), jnp.concatenate([earlier, ones], axis=1))
    carry = jnp.zeros((128, 128), F32)
    values = []
    for b in range(8):
        before = counts[128 * b : 128 * b + 128, :128] + carry
        carry = carry + counts[128 * b : 128 * b + 128, 128:]
        nth = jnp.sum(hots32[b] * before, axis=0, keepdims=True).astype(I32)
        hi = jnp.where(in_lane == nth, part(row_hi, b), 0.0).astype(BF16)
        lo = jnp.where(in_lane == nth, part(row_lo, b), 0.0).astype(BF16)
        values.append(jnp.concatenate([hi, lo], axis=0))
        slot_row[b] = part(bucket, b) * CAP + nth
    halves = nt(jnp.concatenate(hots, axis=1), jnp.concatenate(values, axis=1))
    ask = (halves[:, :128] * 64.0 + halves[:, 128:]).astype(I32)
    for j in range(8):
        ask_send[j] = ask[16 * j : 16 * j + 16]

    pl.semaphore_wait(barrier, 22)
    asks = []
    for j in range(1, 8):
        asks.append(start(remote(ask_send.at[j], ask_mid.at[j], ask1_s.at[j], ask1_r.at[j], zc_plus(j))))
    ask_mid[0] = ask_send[0]

    def widen(begin, end):
        for k in range(begin, end):
            loads[k].wait()

            @pl.loop(0, 16)
            def _(t):
                at = pl.ds(pl.multiple_of(k * 2048 + t * 128, 128), 128)
                tab32[at, :] = tab16[at, :].astype(F32)

    widen(0, 2)
    for copy in asks:
        copy.wait_recv()
    group = lax.broadcasted_iota(I32, (16, 128), 1) // CAP
    merged = ask_mid[0]
    for j in range(1, 8):
        merged = jnp.where(group == j, ask_mid[j], merged)
    for i in range(16):
        ask_mid2[i] = merged[i : i + 1]
    asks2 = []
    for i in range(1, 16):
        asks2.append(start(remote(ask_mid2.at[i], ask_got.at[i], ask2_s.at[i], ask2_r.at[i], yx_plus(i))))
    ask_got[0] = ask_mid2[0]

    widen(2, 4)
    for copy in asks2:
        copy.wait_recv()
    to_smem = pltpu.make_async_copy(ask_got, ask_smem, smem_sem)
    to_smem.start()
    for y, x in FAR:
        at = 8 * CAP * place_of(y, x)
        row_ids[:, at : at + 8 * CAP] = ask_got[y * 4 + x][:, : 8 * CAP]
    to_smem.wait()

    def look_up(i, j, out):
        for c in range(CAP):
            asked = jnp.clip(ask_smem[i, 0, CAP * j + c], 0, ROWS - 1)
            stage[j, pl.ds(c, 1), :] = tab32[pl.ds(asked, 1), :]
        for q in range(3):
            out[q] = stage[j, 4 * q : 4 * q + 4, :].astype(BF16)

    def send_rows(y, x, j):
        r = place_of(y, x) * 8 + j
        look_up(y * 4 + x, j, rows_send.at[r])
        half = 1 - (y + x) % 2
        remote(rows_send.at[r], rows_got.at[r], row_s, row_r.at[half], minus(y * 4 + x, j)).start()

    def column(_, digits):
        for j in ZC_ORDER:
            send_rows(digits % 16 // 4, digits % 4, j)
        return digits // 16

    columns = ODD + EVEN[:-1]
    for part in (columns[:7], columns[7:14]):
        lax.fori_loop(0, 7, column, sum((y * 4 + x) * 16**n for n, (y, x) in enumerate(part)))
    for j in ZC_ORDER:
        send_rows(*columns[14], j)
    for j in ZC_ORDER[:-1]:
        send_rows(0, 0, j)
    look_up(0, 0, rows_got.at[0])

    for b in range(8):
        slot_b = slot_row[b]
        column = jnp.transpose(jnp.broadcast_to(slot_b.astype(F32), (128, 128))).astype(I32)

        @pl.loop(0, 12)
        def _(k):
            at = pl.ds(pl.multiple_of(k * 128, 128), 128)
            pick[128 * b : 128 * b + 128, at] = jnp.where(column == lane + k * 128, 1.0, 0.0).astype(BF16)
            place[at, 128 * b : 128 * b + 128] = jnp.where(sub + k * 128 == slot_b, 1.0, 0.0).astype(BF16)

    for b in range(4):
        part = labels[:, 128 * b : 128 * b + 128].astype(F32)
        label_col[128 * b : 128 * b + 128, :] = jnp.transpose(jnp.broadcast_to(part, (128, 128)))

    rest = pl.ds(1, DEVS - 1)
    sent.append(pltpu.make_async_copy(rows_send.at[rest], rows_send.at[rest], row_s).wait)
    for k in (4, 5):
        loads[k].wait()
    def unpack(got, begin, end):
        @pl.loop(begin // 4, end // 4)
        def _(g):
            for a in range(4):
                for q in range(3):
                    pack[12 * a + 4 * q : 12 * a + 4 * q + 4, :] = got[g * 4 + a, q].astype(F32)
            fetched[pl.ds(pl.multiple_of(g * 48, 16), 48), :] = pack[...].astype(BF16)

    def wait_rows(half):
        at = rows_got.at[halves_at[half]]
        pltpu.make_async_copy(at, at, row_r.at[half]).wait()
        unpack(rows_got, DEVS // 2 * (1 - half), DEVS // 2 * (2 - half))

    halves_at = (pl.ds(DEVS // 2, DEVS // 2), pl.ds(1, DEVS // 2 - 1))
    lower, upper = slice(0, SLOTS // 2), slice(SLOTS // 2, SLOTS)
    wait_rows(0)
    picked[...] = dot(pick[:, upper], fetched[upper, :])
    wait_rows(1)

    local32[...] = jnp.zeros_like(local32)
    head = w_head[...].reshape(1, HID).astype(F32)
    small = [jnp.zeros((1, HID), F32)] * 3
    for m in range(2):
        at = slice(256 * m, 256 * m + 256)
        at2 = slice(PAIRS + 256 * m, PAIRS + 256 * m + 256)
        first = picked[at, :] + dot(pick[at, lower], fetched[lower, :])
        second = picked[at2, :] + dot(pick[at2, lower], fetched[lower, :])
        feat[at, 0:EMB] = first.astype(BF16)
        feat[at, EMB : 2 * EMB] = second.astype(BF16)
        feat[at, 2 * EMB :] = (first * second).astype(BF16)
        pre_first = dot(feat[at, :], w1[...]) + bias_first[...]
        hid1[at, :] = jnp.maximum(pre_first, 0.0).astype(BF16)
        pre_second = dot(hid1[at, :], w2[...]) + bias_second[...]
        hidden_second = jnp.maximum(pre_second, 0.0).astype(BF16).astype(F32)
        logit = jnp.sum(hidden_second * head, axis=1, keepdims=True) + head_bias[0]
        dlogit = 1.0 / (1.0 + jnp.exp(-logit)) - label_col[at, 0:1]
        delta_second = jnp.where(pre_second > 0, dlogit * head, 0.0).astype(BF16)
        del2[at, :] = delta_second
        delta_first = jnp.where(pre_first > 0, nt(delta_second, w2[...]), 0.0).astype(BF16)
        del1[at, :] = delta_first
        small = [
            small[0] + jnp.sum(delta_first.astype(F32), axis=0, keepdims=True),
            small[1] + jnp.sum(delta_second.astype(F32), axis=0, keepdims=True),
            small[2] + jnp.sum(hidden_second * dlogit, axis=0, keepdims=True),
        ]

    for c in range(4):
        for k in range(3):
            local32[unit_place(640 + c), k : k + 1, :] = small[k][:, 128 * c : 128 * c + 128]
        local16[unit_place(640 + c)] = local32[unit_place(640 + c)].astype(BF16)

    here = {"y": my, "x": mx, "z": mz}

    def along(axis, k, other=0):
        at = dict(here)
        at[axis] = (at[axis] + k) % 4
        return device(at["y"], at["x"], at["z"], (mc + other) % 2)

    sibling = device(my, mx, mz, 1 - mc)
    lanes = (("y", "x", "z"), ("x", "z", "y"), ("z", "y", "x"))
    span1, span2 = 4 * PIECE, PIECE
    lane_units = 16 * PIECE

    def core_copy(l):
        at = pl.ds((1 - mc) * (UNITS // 2) + l * lane_units, lane_units)
        return remote(local16.at[at], got_core.at[l], core_s.at[l], core_r.at[l], sibling)

    def rs1_copy(l, k):
        axis = lanes[l][0]
        at = pl.ds((here[axis] + k) % 4 * span1, span1)
        return remote(half0.at[l, at], got1.at[l, k], rs1_s.at[l, k], rs1_r.at[l, k], along(axis, k))

    def rs2_copy(l, k):
        axis = lanes[l][1]
        at = pl.ds((here[axis] + k) % 4 * span2, span2)
        return remote(half1.at[l, at], got2.at[l, k], rs2_s.at[l, k], rs2_r.at[l, k], along(axis, k))

    def x3_copy(l, k):
        axis = lanes[l][2]
        return remote(half2.at[l], got3.at[l, here[axis]], x3_s.at[l, k], x3_r.at[l, k], along(axis, k))

    def unit_at(core, l, one, two=0):
        return core * (UNITS // 2) + l * lane_units + one * span1 + two * span2

    def ag2_copy(l, k):
        a, b = here[lanes[l][0]], here[lanes[l][1]]
        at = gathered.at[pl.ds(unit_at(mc, l, a, b), span2)]
        return remote(at, at, ag2_s.at[l, k], ag2_r.at[l, k], along(lanes[l][1], k))

    def ag1_copy(l, k, other):
        at = gathered.at[pl.ds(unit_at(mc, l, here[lanes[l][0]]), span1)]
        to = along(lanes[l][0], k, other)
        return remote(at, at, ag1_s.at[l, k + 4 * other], ag1_r.at[l, k + 4 * other], to)

    def put(v, value):
        unit = unit_place(v)
        local32[unit] = value
        local16[unit] = value.astype(BF16)

    def put_block(first, grad):
        for n in range(32):
            for c in range(4):
                put(first + n * 4 + c, grad[8 * n : 8 * n + 8, 128 * c : 128 * c + 128])

    for u in range(644, UNITS):
        local16[unit_place(u)] = jnp.zeros((8, 128), BF16)
    for block in range(3):
        put_block(block * 128, tn(feat[:, 256 * block : 256 * block + 256], del1[...]))
        if block == 1:
            start(core_copy(0))
    for block in range(2):
        put_block(UNITS_FIRST + block * 128, tn(hid1[:, 256 * block : 256 * block + 256], del2[...]))
        start(core_copy(1 + block))


    for m in range(2):
        at = slice(256 * m, 256 * m + 256)
        grad_input = nt(del1[at, :], w1[...])
        grad_product = grad_input[:, 2 * EMB :]
        grad_one = grad_input[:, :EMB] + grad_product * feat[at, EMB : 2 * EMB].astype(F32)
        grad_two = grad_input[:, EMB : 2 * EMB] + grad_product * feat[at, 0:EMB].astype(F32)
        one_hot_grads[256 * m : 256 * m + 256, :] = grad_one.astype(BF16)
        one_hot_grads[PAIRS + 256 * m : PAIRS + 256 * m + 256, :] = grad_two.astype(BF16)

    @pl.loop(0, 4)
    def _(k):
        at = pl.ds(pl.multiple_of(k * 384, 128), 384)
        out32[...] = dot(place[at, :], one_hot_grads[...])
        for r in range(32):
            for q in range(3):
                grads_send[k * 32 + r, q] = out32[12 * r + 4 * q : 12 * r + 4 * q + 4, :].astype(BF16)

    def send_grads(half, columns):
        for y, x in columns:
            for j in ZC_ORDER:
                r = place_of(y, x) * 8 + j
                if r:
                    copy = remote(
                        grads_send.at[r], incoming.at[r], grad_s.at[half], grad_r.at[half], plus(y * 4 + x, j)
                    )
                    copy.start()

    def sent_grads(half):
        at = grads_send.at[halves_at[half]]
        sent.append(pltpu.make_async_copy(at, at, grad_s.at[half]).wait)

    incoming[0] = grads_send[0]
    def wait_grads(half):
        at = incoming.at[halves_at[half]]
        pltpu.make_async_copy(at, at, grad_r.at[half]).wait()
        unpack(incoming, DEVS // 2 * (1 - half), DEVS // 2 * (2 - half))

    def update(half, begin, end):
        slots = slice(SLOTS // 2 * (1 - half), SLOTS // 2 * (2 - half))
        for base in range(begin * 1024, end * 1024, 1024):
            here_row = lax.broadcasted_iota(I32, (1024, SLOTS // 2), 0) + base
            hot_rows[...] = jnp.where(here_row == row_ids[:, slots], 1.0, 0.0).astype(BF16)
            at = slice(base, base + 1024)
            tab32[at, :] = tab32[at, :] - 8.0 * dot(hot_rows[...], fetched[slots, :])

    for l in range(3):
        core_copy(l).wait_recv()

        @pl.loop(0, 16)
        def _(t):
            at = pl.ds(t * PIECE, PIECE)
            total = (
                local32[pl.ds(mc * (UNITS // 2) + l * lane_units + t * PIECE, PIECE)]
                + got_core[l, at].astype(F32)
            )
            sum0[l, at] = total
            half0[l, at] = total.astype(BF16)

        for k in (2, 1, 3):
            start(rs1_copy(l, k))
    send_grads(0, ODD)
    sent_grads(0)

    for l in range(3):
        for k in range(1, 4):
            rs1_copy(l, k).wait_recv()
        for t in range(4):
            at = pl.ds(t * PIECE, PIECE)
            total = sum0[l, pl.ds(here[lanes[l][0]] * span1 + t * PIECE, PIECE)]
            for k in range(1, 4):
                total = total + got1[l, k, at].astype(F32)
            sum1[l, at] = total
            half1[l, at] = total.astype(BF16)
        for k in (2, 1, 3):
            start(rs2_copy(l, k))
    send_grads(1, EVEN[:4])

    wait_grads(0)
    update(0, 0, 3)
    for l in range(3):
        for k in range(1, 4):
            rs2_copy(l, k).wait_recv()
        total = sum1[l, pl.ds(here[lanes[l][1]] * span2, PIECE)]
        for k in range(1, 4):
            total = total + got2[l, k].astype(F32)
        half2[l] = total.astype(BF16)
        got3[l, here[lanes[l][2]]] = total.astype(BF16)
        for k in (2, 1, 3):
            start(x3_copy(l, k))
    send_grads(1, EVEN[4:])
    update(0, 3, 6)
    for l in range(3):
        for k in range(1, 4):
            x3_copy(l, k).wait_recv()
        total = got3[l, 0].astype(F32)
        for a in range(1, 4):
            total = total + got3[l, a].astype(F32)
        gathered[pl.ds(unit_at(mc, l, here[lanes[l][0]], here[lanes[l][1]]), PIECE)] = total.astype(BF16)
        for k in (2, 1, 3):
            start(ag2_copy(l, k))
    sent_grads(1)
    early, sent[:] = list(sent), []
    update(0, 6, 8)
    for l in range(3):
        for k in range(1, 4):
            ag2_copy(l, k).wait_recv()
        for k, other in AG1_ORDER:
            start(ag1_copy(l, k, other))
    flush(early)
    wait_grads(1)
    update(1, 0, 8)
    for l in range(3):
        for k, other in AG1_ORDER:
            ag1_copy(l, k, other).wait_recv()

    flush(sent)


def step(owners, rows, labels, table, w_first, bias_first, w_second, bias_second, w_head, head_bias):
    vmem = pl.BlockSpec(memory_space=pltpu.VMEM)
    any_ = pl.BlockSpec(memory_space=pl.ANY)
    dma = pltpu.SemaphoreType.DMA
    scratch = [
        pltpu.VMEM((DEVS, 3, 4, EMB), BF16),
        pltpu.VMEM((1, SLOTS), I32),
        pltpu.VMEM((1024, SLOTS // 2), BF16),
        pltpu.VMEM((ROWS, EMB), BF16),
        pltpu.VMEM((IN, HID), BF16),
        pltpu.VMEM((HID, HID), BF16),
        pltpu.VMEM((8, 16, 128), I32),
        pltpu.VMEM((8, 16, 128), I32),
        pltpu.VMEM((16, 1, 128), I32),
        pltpu.VMEM((16, 1, 128), I32),
        pltpu.SMEM((16, 1, 128), I32),
        pltpu.VMEM((8, 1, 128), I32),
        pltpu.VMEM((PAIRS, 128), F32),
        pltpu.VMEM((2 * PAIRS, SLOTS), BF16),
        pltpu.VMEM((2 * PAIRS, EMB), F32),
        pltpu.VMEM((SLOTS, 2 * PAIRS), BF16),
        pltpu.VMEM((8, 16, EMB), F32),
        pltpu.VMEM((DEVS, 3, 4, EMB), BF16),
        pltpu.VMEM((DEVS, 3, 4, EMB), BF16),
        pltpu.VMEM((48, EMB), F32),
        pltpu.VMEM((SLOTS, EMB), BF16),
        pltpu.VMEM((PAIRS, IN), BF16),
        pltpu.VMEM((PAIRS, HID), BF16),
        pltpu.VMEM((PAIRS, HID), BF16),
        pltpu.VMEM((PAIRS, HID), BF16),
        pltpu.VMEM((2 * PAIRS, EMB), BF16),
        pltpu.VMEM((384, EMB), F32),
        pltpu.VMEM((DEVS, 3, 4, EMB), BF16),
        pltpu.VMEM((UNITS, 8, 128), F32),
        pltpu.VMEM((UNITS, 8, 128), BF16),
        pltpu.VMEM((3, 16 * PIECE, 8, 128), BF16),
        pltpu.VMEM((3, 16 * PIECE, 8, 128), F32),
        pltpu.VMEM((3, 16 * PIECE, 8, 128), BF16),
        pltpu.VMEM((3, 4, 4 * PIECE, 8, 128), BF16),
        pltpu.VMEM((3, 4 * PIECE, 8, 128), F32),
        pltpu.VMEM((3, 4 * PIECE, 8, 128), BF16),
        pltpu.VMEM((3, 4, PIECE, 8, 128), BF16),
        pltpu.VMEM((3, PIECE, 8, 128), BF16),
        pltpu.VMEM((3, 4, PIECE, 8, 128), BF16),
        dma((6,)), dma((8,)), dma((8,)), dma((16,)), dma((16,)), dma, dma, dma((2,)), dma((2,)), dma((2,)),
        dma((3,)), dma((3,)), dma((3, 4)), dma((3, 4)), dma((3, 4)), dma((3, 4)), dma((3, 4)), dma((3, 4)),
        dma((3, 4)), dma((3, 4)), dma((3, 8)), dma((3, 8)),
    ]
    return pl.pallas_call(
        step_kernel,
        out_shape=(pltpu.VMEM((ROWS, EMB), F32), pltpu.VMEM((UNITS, 8, 128), BF16)),
        in_specs=[vmem, vmem, vmem, any_, any_, vmem, any_, vmem, vmem, pl.BlockSpec(memory_space=pltpu.SMEM)],
        out_specs=(vmem, vmem),
        scratch_shapes=scratch,
        compiler_params=pltpu.CompilerParams(
            collective_id=0, has_side_effects=True, vmem_limit_bytes=VMEM_STEP
        ),
        name="exchange_and_mlp",
    )(owners, rows, labels, table, w_first, bias_first, w_second, bias_second, w_head, head_bias)


def finish_kernel(
    table, units, new_table, grad_first, grad_second, grad_small, first32, second32, table_sem, grad_sem
):
    parts = [
        pltpu.make_async_copy(
            table.at[pl.ds(k * 1024, 1024)], new_table.at[pl.ds(k * 1024, 1024)], table_sem.at[k]
        )
        for k in range(8)
    ]
    for part in parts:
        part.start()
    for array, out, first_unit in ((first32, grad_first, 0), (second32, grad_second, UNITS_FIRST)):

        @pl.loop(0, array.shape[0] // 32)
        def _(t):
            for u in range(4):
                at = pl.ds(pl.multiple_of(t * 32 + u * 8, 8), 8)
                for c in range(4):
                    array[at, 128 * c : 128 * c + 128] = units[unit_place(first_unit + t * 16) + u * 4 + c].astype(F32)

        part = pltpu.make_async_copy(array, out, grad_sem.at[len(parts) - 8])
        part.start()
        parts.append(part)
    for c in range(4):
        grad_small[:, 128 * c : 128 * c + 128] = units[unit_place(640 + c)].astype(F32)[0:3]
    for part in parts:
        part.wait()


def finish(table, units):
    vmem = pl.BlockSpec(memory_space=pltpu.VMEM)
    any_ = pl.BlockSpec(memory_space=pl.ANY)
    return pl.pallas_call(
        finish_kernel,
        in_specs=[vmem, vmem],
        out_specs=(any_, any_, any_, vmem),
        out_shape=(
            jax.ShapeDtypeStruct((ROWS, EMB), F32),
            jax.ShapeDtypeStruct((IN, HID), F32),
            jax.ShapeDtypeStruct((HID, HID), F32),
            jax.ShapeDtypeStruct((3, HID), F32),
        ),
        scratch_shapes=[
            pltpu.VMEM((IN, HID), F32),
            pltpu.VMEM((HID, HID), F32),
            pltpu.SemaphoreType.DMA((8,)),
            pltpu.SemaphoreType.DMA((2,)),
        ],
        compiler_params=pltpu.CompilerParams(vmem_limit_bytes=8 << 20),
        name="write_out",
    )(pltpu.with_memory_space_constraint(table, pltpu.VMEM), pltpu.with_memory_space_constraint(units, pltpu.VMEM))


def on_device(
    node_table, owners, local_rows, labels, w_first, bias_first, w_second, bias_second, w_head, head_bias
):
    table, units = step(
        owners.T, local_rows.T, labels.reshape(1, PAIRS), node_table,
        w_first, bias_first.reshape(1, HID), w_second, bias_second.reshape(1, HID), w_head, head_bias,
    )
    return finish(table, units)


def solution(mesh):
    in_specs = (P("dev", None), P("dev", None), P("dev", None), P("dev"), P(), P(), P(), P(), P(), P())
    out_specs = (P("dev", None), P(), P(), P())
    return jax.shard_map(on_device, mesh=mesh, in_specs=in_specs, out_specs=out_specs, check_vma=False)
```
